768 devices in a mesh: dp: 32 (over y_hi, x, core), pipe: 24 (over y_lo, z).
Axes of the slice: x: 4, y: 8 (y_hi: 4, y_lo: 2; y = y_hi * 2 + y_lo), z: 12, core: 2. Of those that a mesh axis runs over, the one named last changes fastest.
Arguments:
- activations: bfloat16 [24, 16384, 1024], P('pipe', 'dp'), may hold values from -6 to 6
- out_grad: bfloat16 [16384, 1024], P('dp'), may hold values from -6 to 6
- w_up: bfloat16 [24, 2, 1024, 512], P('pipe'), may hold values from -0.1875 to 0.1875
- w_down: bfloat16 [24, 2, 512, 1024], P('pipe'), may hold values from -0.25 to 0.25
- mod_scale: float32 [24, 32, 1024], P('pipe'), may hold values from -1.2 to 1.2
- mod_gate: float32 [24, 32, 1024], P('pipe'), may hold values from -4 to 4
- expert_ids: int32 [24, 16384, 4], P('pipe', 'dp'), may hold values from 0 to 63, as said below
- gate_prob: float32 [24, 16384, 4], P('pipe', 'dp'), may hold values from 0.05 to 0.6
- bucket: int32 [16384], P('dp'), may hold values from 0 to 31
Outputs:
- input_grad: bfloat16 [24, 16384, 1024], P('pipe', 'dp')
- grad_up: float32 [24, 2, 1024, 512], P('pipe', None, 'dp')
- grad_down: float32 [24, 2, 512, 1024], P('pipe', None, None, 'dp')
The draws below stay inside these ranges and needn't reach their ends.
Inputs may be any that keep to these rules, and one draw needn't show every extreme that they name: `expert_ids`: each token names 4 different experts at each layer. Each expert below 2 is named by at most 16 tokens of each micro-batch (aligned block of 64 tokens) at each layer, by exactly 16 in some micro-batch of every layer, and by at least half of 16 in every micro-batch.
All inputs are finite; a program needn't handle non-finite values.
Results may differ from the reference program's by a relative error of at most 0.014.
Values may be sent and summed in bfloat16 or wider, within the bound.
No kernel may reach another device: no remote copies, remote signals or barrier semaphores. Data moves between devices by JAX's collectives and lax.ppermute only.
A program may use at most 64 MiB of HBM per device.

```python
import jax
import jax.numpy as jnp
from jax import lax

D = 1024
H = 512
EXPERTS = 64
EXP_LOC = 2
TOPK = 4
BUCKETS = 32
TOK_MB = 64
CAP = 16
TOKENS = 16384
N_PIPE = 24


def draw_expert_ids(key, part):
    key = jax.random.fold_in(key, 7)
    keys = jax.random.split(key, 6)
    blocks = TOKENS // TOK_MB
    spare = EXPERTS - EXP_LOC
    base = jax.random.randint(keys[0], (N_PIPE, TOKENS), 0, spare)
    stride = jax.random.randint(keys[1], (N_PIPE, TOKENS), 1, (spare - 1) // 3 + 1)
    ranks = jnp.arange(TOPK, dtype=jnp.int32)
    others = EXP_LOC + (base[:, :, None] + ranks[None, None, :] * stride[:, :, None]) % spare
    counts = jax.random.randint(keys[2], (N_PIPE, EXP_LOC, blocks), (CAP + 1) // 2, CAP + 1)
    fullest = jax.random.randint(keys[3], (N_PIPE, EXP_LOC, 1), 0, blocks)
    counts = jnp.where(jnp.arange(blocks, dtype=jnp.int32)[None, None, :] == fullest, CAP, counts)
    perm_keys = jax.random.split(keys[4], N_PIPE * EXP_LOC * blocks)
    orders = jax.vmap(lambda one_key: jax.random.permutation(one_key, TOK_MB))(perm_keys)
    orders = orders.reshape(N_PIPE, EXP_LOC, blocks, TOK_MB)
    picked = (orders < counts[:, :, :, None]).reshape(N_PIPE, EXP_LOC, TOKENS)
    picked = jnp.transpose(picked, (0, 2, 1))
    picked = jnp.concatenate([picked, jnp.zeros((N_PIPE, TOKENS, TOPK - EXP_LOC), bool)], axis=2)
    slots = jnp.where(picked, ranks[None, None, :], others)
    turn = jax.random.randint(keys[5], (N_PIPE, TOKENS, 1), 0, TOPK)
    order = (ranks[None, None, :] + turn) % TOPK
    routes = jnp.take_along_axis(slots, order, axis=2)
    return routes.astype(jnp.int32)


def with_ends(values, rng, low, top_value):
    longest = values.shape.index(max(values.shape))
    spots = []
    for shift in (0, 1):
        where = [jax.random.randint(jax.random.fold_in(rng, axis), (), 0, length) for axis, length in enumerate(values.shape)]
        where[longest] = (where[longest] + shift) % values.shape[longest]
        spots.append(tuple(where))
    return values.at[spots[0]].set(low).at[spots[1]].set(top_value)


def levels(stream_key, extent, cuts, least, high):
    def one(dim, parts):
        draws = jax.random.uniform(jax.random.fold_in(jax.random.fold_in(stream_key, 6), dim), (parts,), jnp.float32, least / len(cuts), high / len(cuts))
        return jnp.repeat(jnp.exp(draws), extent[dim] // parts).reshape((-1,) + (1,) * (len(extent) - dim - 1))

    loudness = one(*cuts[0])
    for cut in cuts[1:]:
        loudness = loudness * one(*cut)
    return loudness


def bell_draw(key, dims, spread, most, pieces=(), kind=jnp.bfloat16):
    entries = jax.random.normal(key, dims, jnp.float32) * spread
    if len(pieces) > 0:
        entries = levels(key, dims, pieces, -0.22, 0.18) * entries
    return jnp.clip(entries, min=-most, max=most).astype(kind)


def setup_inputs(seed: int = 0) -> dict:
    arg_keys = jax.random.split(jax.random.key(seed), 10)
    return {
        "activations": bell_draw(arg_keys[0], (N_PIPE, TOKENS, D), 1.0, 6.0, ((0, 24), (1, 32))),
        "out_grad": bell_draw(arg_keys[1], (TOKENS, D), 1.0, 6.0, ((0, 32),)),
        "w_up": bell_draw(arg_keys[2], (N_PIPE, EXP_LOC, D, H), D ** -0.5, 0.1875, ((0, 24),)),
        "w_down": bell_draw(arg_keys[3], (N_PIPE, EXP_LOC, H, D), H ** -0.5, 0.25, ((0, 24),)),
        "mod_scale": bell_draw(arg_keys[4], (N_PIPE, BUCKETS, D), 0.3, 1.2, ((0, 24),), jnp.float32),
        "mod_gate": bell_draw(arg_keys[5], (N_PIPE, BUCKETS, D), 1.0, 4.0, ((0, 24),), jnp.float32),
        "expert_ids": draw_expert_ids(jax.random.fold_in(arg_keys[9], 71), 0),
        "gate_prob": jnp.clip(0.05 + 0.55 * jax.random.uniform(arg_keys[7], (N_PIPE, TOKENS, TOPK), jnp.float32) ** levels(arg_keys[7], (N_PIPE, TOKENS, TOPK), ((0, 24), (1, 32)), -0.2, 0.2), 0.05, 0.6),
        "bucket": with_ends(jax.random.randint(arg_keys[8], (TOKENS,), 0, BUCKETS), jax.random.fold_in(arg_keys[8], 1), 0, BUCKETS - 1).astype(jnp.int32),
    }


EPSILON = 1e-06
HIGHEST = lax.Precision.HIGHEST

def gelu_pair(values):
    return jax.jvp(jax.nn.gelu, (values,), (jnp.ones_like(values),))

def layer_backward(layer_in, grad_out, up_mats, down_mats, scale_table, gate_table, routes, probs, buckets):
    layer_f = layer_in.astype(jnp.float32)
    centred = layer_f - lax.optimization_barrier(jnp.mean(layer_f, axis=-1, keepdims=True))
    inv_std = lax.rsqrt(lax.optimization_barrier(jnp.mean(centred * centred, axis=-1, keepdims=True)) + EPSILON)
    normed = centred * inv_std
    scale_rows = 1.0 + scale_table[buckets]
    gate_rows = gate_table[buckets]
    expert_in = (normed * scale_rows).astype(jnp.bfloat16)
    scaled = gate_rows * grad_out.astype(jnp.float32)
    slot_ids = jnp.arange(CAP, dtype=jnp.int32)
    token_term = jnp.zeros(layer_f.shape, jnp.float32)
    up_parts = []
    down_parts = []
    for expert in range(EXP_LOC):
        up_mat = up_mats[expert]
        down_mat = down_mats[expert]
        chosen = routes == expert
        routed = jnp.any(chosen, axis=-1)
        token_gate = lax.optimization_barrier(jnp.sum(jnp.where(chosen, probs, 0.0), axis=-1))
        position = jnp.cumsum(routed.astype(jnp.int32), axis=1) - 1
        dispatch = ((position[:, None, :] == slot_ids[None, :, None]) & routed[:, None, :]).astype(jnp.float32)
        slot_rows = jnp.einsum('bct,btd->bcd', dispatch, expert_in.astype(jnp.float32), precision=HIGHEST).astype(jnp.bfloat16)
        pre_act = jnp.einsum('bcd,dh->bch', slot_rows.astype(jnp.float32), up_mat.astype(jnp.float32))
        act_val, act_slope = gelu_pair(pre_act)
        hidden = act_val.astype(jnp.bfloat16)
        slot_gate = jnp.einsum('bct,bt->bc', dispatch, token_gate, precision=HIGHEST)
        out_slots = (slot_gate[:, :, None] * jnp.einsum('bct,btd->bcd', dispatch, scaled, precision=HIGHEST)).astype(jnp.bfloat16)
        hid_grad = jnp.einsum('bcd,hd->bch', out_slots.astype(jnp.float32), down_mat.astype(jnp.float32))
        pre_grad = (hid_grad * act_slope).astype(jnp.bfloat16)
        in_slots = jnp.einsum('bch,dh->bcd', pre_grad.astype(jnp.float32), up_mat.astype(jnp.float32))
        token_term = token_term + jnp.einsum('bct,bcd->btd', dispatch, in_slots, precision=HIGHEST)
        up_parts.append(jnp.einsum('bcd,bch->dh', slot_rows.astype(jnp.float32), pre_grad.astype(jnp.float32)))
        down_parts.append(jnp.einsum('bch,bcd->hd', hidden.astype(jnp.float32), out_slots.astype(jnp.float32)))
    varied = token_term * scale_rows
    lifted = varied - lax.optimization_barrier(jnp.mean(varied, axis=-1, keepdims=True)) - normed * lax.optimization_barrier(jnp.mean(varied * normed, axis=-1, keepdims=True))
    grad_in = (grad_out.astype(jnp.float32) + inv_std * lifted).astype(jnp.bfloat16)
    return (grad_in, jnp.stack(up_parts), jnp.stack(down_parts))

def reference(activations, out_grad, w_up, w_down, mod_scale, mod_gate, expert_ids, gate_prob, bucket):
    blocks = TOKENS // TOK_MB
    buckets = bucket.reshape(blocks, TOK_MB)
    grad_out = out_grad.reshape(blocks, TOK_MB, D)
    grads_list = []
    ups_list = []
    downs_list = []
    for layer_no in reversed(range(N_PIPE)):
        grad_out, up_part, down_part = layer_backward(activations[layer_no].reshape(blocks, TOK_MB, D), grad_out, w_up[layer_no], w_down[layer_no], mod_scale[layer_no], mod_gate[layer_no], expert_ids[layer_no].reshape(blocks, TOK_MB, TOPK), gate_prob[layer_no].reshape(blocks, TOK_MB, TOPK), buckets)
        grads_list.append(grad_out.reshape(TOKENS, D))
        ups_list.append(up_part)
        downs_list.append(down_part)
    input_grad = jnp.stack(grads_list[::-1])
    return (input_grad, jnp.stack(ups_list[::-1]), jnp.stack(downs_list[::-1]))
```

```python
import functools

import jax
import jax.numpy as jnp
from jax import lax
from jax.experimental import pallas as pl
from jax.experimental.pallas import tpu as pltpu
from jax.sharding import PartitionSpec as P

TOK_MB = 64
CAP = 16
EPSILON = 1e-06
F32 = jnp.float32
BF16 = jnp.bfloat16
VMEM_LIMIT = 24 * 1024 * 1024
STEP_LIMIT = 6 * 1024 * 1024


def in_vmem(value):
    return pltpu.with_memory_space_constraint(value, pltpu.VMEM)


def kept_shape(shape, dtype):
    return pltpu.VMEM(shape, dtype)


def vmem_specs(count):
    return [pl.BlockSpec(memory_space=pltpu.VMEM)] * count


def three_parts(table):
    high = table.astype(BF16)
    rest = table - high.astype(F32)
    middle = rest.astype(BF16)
    low = (rest - middle.astype(F32)).astype(BF16)
    return jnp.concatenate([high, middle, low], axis=0)


def prepare_kernel(
    act_ref,
    ids_ref,
    prob_ref,
    bucket_ref,
    scale_table_ref,
    gate_table_ref,
    up_ref,
    take_ref,
    place_ref,
    gate_ref,
    scale_ref,
    normed_ref,
    slope_ref,
    hidden_ref,
    rows_ref,
    *_store_refs,
):
    tokens = act_ref.shape[0]
    experts = up_ref.shape[0]
    slots = experts * CAP
    features = act_ref.shape[1]
    ids = ids_ref[...]
    prob = prob_ref[...]
    bucket = bucket_ref[...].astype(F32)
    lane = lax.broadcasted_iota(jnp.int32, (1, tokens), 1) % TOK_MB
    slot_no = (lax.broadcasted_iota(jnp.int32, (CAP, tokens), 0) + 1).astype(F32)
    hits = []
    gates = []
    for expert in range(experts):
        chosen = ids == expert
        routed = jnp.max(jnp.where(chosen, 1.0, 0.0), axis=0, keepdims=True)
        token_gate = jnp.sum(jnp.where(chosen, prob, 0.0), axis=0, keepdims=True)
        place = routed
        step = 1
        while step < TOK_MB:
            place = place + jnp.where(lane >= step, pltpu.roll(place, step, 1), 0.0)
            step *= 2
        hit = jnp.where((place == slot_no) & (routed > 0.0), 1.0, 0.0)
        hits.append(hit)
        gates.append(hit * token_gate)
    take = jnp.concatenate(hits, axis=0)
    gates = jnp.concatenate(gates, axis=0)
    buckets = take * bucket
    tables = three_parts(scale_table_ref[...]), three_parts(gate_table_ref[...])
    entries = scale_table_ref.shape[0]
    wide = lax.broadcasted_iota(jnp.int32, (slots, 2 * TOK_MB), 1)
    eye = jnp.where(
        lax.broadcasted_iota(jnp.int32, (TOK_MB, 2 * TOK_MB), 0)
        == lax.broadcasted_iota(jnp.int32, (TOK_MB, 2 * TOK_MB), 1),
        1.0,
        0.0,
    )
    entry_no = lax.broadcasted_iota(jnp.int32, (slots, 3 * entries), 1) % entries
    for block in range(tokens // TOK_MB):
        pair = slice(block // 2 * 2 * TOK_MB, (block // 2 + 1) * 2 * TOK_MB)
        inside = (wide < TOK_MB) if block % 2 == 0 else (wide >= TOK_MB)
        block_take = jnp.where(inside, take[:, pair], 0.0)
        slot_gate = jnp.sum(jnp.where(inside, gates[:, pair], 0.0), axis=1, keepdims=True)
        slot_bucket = jnp.sum(jnp.where(inside, buckets[:, pair], 0.0), axis=1, keepdims=True)
        raw = jnp.dot(block_take.astype(BF16), act_ref[pair, :], preferred_element_type=F32)
        first = block_take if block % 2 == 0 else pltpu.roll(block_take, TOK_MB, 1)
        take_ref[block] = first.astype(BF16)
        stacked = jnp.concatenate([first, first, eye], axis=0)
        place_ref[block] = jnp.transpose(stacked)[:TOK_MB, :].astype(BF16)
        picked = jnp.where(slot_bucket.astype(jnp.int32) == entry_no, 1.0, 0.0).astype(BF16)
        scale_rows = 1.0 + jnp.dot(picked, tables[0], preferred_element_type=F32)
        gate_rows = jnp.dot(picked, tables[1], preferred_element_type=F32)
        gate_ref[block] = slot_gate * gate_rows
        centred = raw - jnp.mean(raw, axis=-1, keepdims=True)
        inv_std = lax.rsqrt(jnp.mean(centred * centred, axis=-1, keepdims=True) + EPSILON)
        normed = centred * inv_std
        normed_ref[block] = normed
        scale_ref[block] = scale_rows * inv_std
        inputs = (normed * scale_rows).astype(BF16)
        for expert in range(experts):
            rows_ref[expert, block * CAP : (block + 1) * CAP, :] = inputs[
                expert * CAP : (expert + 1) * CAP, :
            ]
    for expert in range(experts):
        pre_act = jnp.dot(rows_ref[expert], up_ref[expert], preferred_element_type=F32)
        root = 0.7978845608028654
        square = pre_act * pre_act
        bend = jnp.tanh(root * (pre_act + 0.044715 * (square * pre_act)))
        half = 0.5 * (1.0 + bend)
        hidden_ref[expert] = (pre_act * half).astype(BF16)
        slope = half + 0.5 * pre_act * (1.0 - bend * bend) * (root * (1.0 + 0.134145 * square))
        slope_ref[expert] = slope.reshape(slope_ref.shape[1:])


def prepare(act, ids, prob, bucket, scale_table, gate_table, up_mats):
    tokens, features = act.shape
    experts, _, width = up_mats.shape
    blocks = tokens // TOK_MB
    slots = experts * CAP
    return pl.pallas_call(
        prepare_kernel,
        out_shape=(
            kept_shape((blocks, slots, 2 * TOK_MB), BF16),
            kept_shape((blocks, TOK_MB, 2 * slots + TOK_MB), BF16),
            kept_shape((blocks, slots, features), F32),
            kept_shape((blocks, slots, features), F32),
            kept_shape((blocks, slots, features), F32),
            kept_shape((experts, blocks, CAP, width), F32),
            kept_shape((experts, blocks * CAP, width), BF16),
            kept_shape((experts, blocks * CAP, features), BF16),
            kept_shape((blocks, TOK_MB, features), BF16),
            kept_shape((experts, blocks, CAP, features), BF16),
            kept_shape((experts, blocks, CAP, width), BF16),
        ),
        in_specs=vmem_specs(7),
        out_specs=tuple(vmem_specs(11)),
        compiler_params=pltpu.CompilerParams(vmem_limit_bytes=VMEM_LIMIT),
    )(act, ids, prob, bucket, scale_table, gate_table, up_mats)


def step_kernel(
    round_no,
    parity,
    given_ref,
    top_ref,
    take_ref,
    place_ref,
    gate_ref,
    scale_ref,
    normed_ref,
    slope_ref,
    down_ref,
    up_ref,
    _grad_in,
    _outs_in,
    _pres_in,
    sent_ref,
    grad_ref,
    outs_ref,
    pres_ref,
):
    experts = down_ref.shape[0]
    blocks = take_ref.shape[0]
    depth = lax.axis_size("pipe") - 1 - lax.axis_index("pipe")
    block = round_no - depth

    @pl.when((depth % 2 == parity) & (block >= 0) & (block < blocks))
    def _():
        grad_out = jnp.where(depth == 0, top_ref[block], given_ref[...])
        gathered = jnp.dot(take_ref[block][:, :TOK_MB], grad_out, preferred_element_type=F32)
        outs = (gate_ref[block] * gathered).astype(BF16)
        back = []
        for expert in range(experts):
            rows = slice(expert * CAP, (expert + 1) * CAP)
            outs_ref[expert, block] = outs[rows, :]
            hid_grad = turned_dot(outs[rows, :], down_ref[expert])
            pres = (hid_grad * slope_ref[expert, block]).astype(BF16)
            pres_ref[expert, block] = pres
            back.append(turned_dot(pres, up_ref[expert]))
        varied = jnp.concatenate(back, axis=0) * scale_ref[block]
        normed = normed_ref[block]
        lifted = (
            varied
            - jnp.mean(varied, axis=-1, keepdims=True)
            - normed * jnp.mean(varied * normed, axis=-1, keepdims=True)
        )
        high = lifted.astype(BF16)
        low = (lifted - high.astype(F32)).astype(BF16)
        parts = jnp.concatenate([high, low, grad_out], axis=0)
        grad_in = jnp.dot(place_ref[block], parts, preferred_element_type=F32).astype(BF16)
        sent_ref[...] = grad_in
        grad_ref[block] = grad_in


def turned_dot(left, right):
    return lax.dot_general(left, right, (((1,), (1,)), ((), ())), preferred_element_type=F32)


def run_step(round_no, parity, given, fixed, stores):
    out_shape = (given,) + stores
    count = 1 + len(fixed)
    return pl.pallas_call(
        functools.partial(step_kernel, round_no, parity),
        out_shape=tuple(kept_shape(v.shape, v.dtype) for v in out_shape),
        in_specs=vmem_specs(count + len(stores)),
        out_specs=tuple(vmem_specs(len(out_shape))),
        input_output_aliases={count + i: 1 + i for i in range(len(stores))},
        compiler_params=pltpu.CompilerParams(vmem_limit_bytes=STEP_LIMIT),
    )(in_vmem(given), *[in_vmem(v) for v in fixed], *[in_vmem(v) for v in stores])


def run_chain(prepared, out_grad, w_up, w_down):
    take, place, gate, scale, normed, slope, hidden, rows, *stores = prepared
    blocks = take.shape[0]
    experts, width, features = w_down.shape
    top = out_grad.reshape(blocks, TOK_MB, features)
    fixed = (top, take, place, gate, scale, normed, slope, w_down, w_up)
    sections = lax.axis_size("pipe")
    stores = tuple(stores)
    given = [top[0], top[0]]
    for round_no in range(sections + blocks - 1):
        for stream in (0, 1):
            parity = (round_no + stream) % 2
            senders = [
                depth
                for depth in range(sections)
                if depth % 2 == parity and 0 <= round_no - depth < blocks
            ]
            if not senders:
                continue
            sent, *stores = run_step(round_no, parity, given[stream], fixed, tuple(stores))
            pairs = [(sections - 1 - d, sections - 2 - d) for d in senders if d < sections - 1]
            if pairs:
                given[stream] = lax.ppermute(sent, "pipe", pairs)
    return tuple(stores)


def grads_kernel(rows_ref, pres_ref, hidden_ref, outs_ref, keep_ref, send_ref):
    experts, blocks, cap, features = outs_ref.shape
    chunk = keep_ref.shape[2]
    tile = 256
    core = lax.axis_index("dp") % 2
    terms = []
    for e in range(experts):
        terms.append((rows_ref[e], pres_ref[e].reshape(blocks * cap, -1)))
    for e in range(experts):
        terms.append((outs_ref[e].reshape(blocks * cap, features), hidden_ref[e]))
    for number, (left, right) in enumerate(terms):
        for start in range(0, features, tile):
            part = lax.dot_general(
                left[:, start : start + tile],
                right,
                (((0,), (0,)), ((), ())),
                preferred_element_type=F32,
            ).astype(BF16)
            for pair in range(tile // (2 * chunk)):
                place = start // (2 * chunk) + pair
                low = part[2 * pair * chunk : (2 * pair + 1) * chunk]
                high = part[(2 * pair + 1) * chunk : (2 * pair + 2) * chunk]
                keep_ref[place, number] = jnp.where(core == 0, low, high)
                send_ref[place, number] = jnp.where(core == 0, high, low)


def expert_grads(rows, pres, hidden, outs, owners):
    experts, _, features = rows.shape
    width = pres.shape[-1]
    shape = (owners // 2, 2 * experts, features // owners, width)
    return pl.pallas_call(
        grads_kernel,
        out_shape=(kept_shape(shape, BF16),) * 2,
        in_specs=vmem_specs(4),
        out_specs=tuple(vmem_specs(2)),
        compiler_params=pltpu.CompilerParams(vmem_limit_bytes=VMEM_LIMIT),
    )(in_vmem(rows), in_vmem(pres), in_vmem(hidden), in_vmem(outs))


def split_x_kernel(keep_ref, came_ref, *part_refs):
    along_x = len(part_refs)
    my_x = lax.axis_index("dp") // 2 % along_x
    for ahead, part_ref in enumerate(part_refs):
        column = (my_x + ahead) % along_x
        for row in range(part_ref.shape[0]):
            place = row * along_x + column
            part_ref[row] = (keep_ref[place].astype(F32) + came_ref[place].astype(F32)).astype(BF16)


def split_y_kernel(along_x, own_ref, *refs):
    came_refs, part_refs = refs[: along_x - 1], refs[along_x - 1 :]
    along_y = len(part_refs)
    my_y = lax.axis_index("dp") // (2 * along_x)
    for ahead, part_ref in enumerate(part_refs):
        row = (my_y + ahead) % along_y
        total = own_ref[row].astype(F32)
        for came_ref in came_refs:
            total = total + came_ref[row].astype(F32)
        part_ref[...] = total.astype(part_ref.dtype)


def finish_kernel(own_ref, *refs):
    came_refs, (up_ref, down_ref) = refs[:-2], refs[-2:]
    experts = up_ref.shape[0]
    for number in range(2 * experts):
        total = own_ref[number]
        for came_ref in came_refs:
            total = total + came_ref[number].astype(F32)
        if number < experts:
            up_ref[number] = total
        else:
            down_ref[number - experts] = jnp.transpose(total)


def call_in_vmem(kernel, out_shape, *values):
    return pl.pallas_call(
        kernel,
        out_shape=out_shape,
        in_specs=vmem_specs(len(values)),
        out_specs=tuple(vmem_specs(len(out_shape))),
        compiler_params=pltpu.CompilerParams(vmem_limit_bytes=VMEM_LIMIT),
    )(*[in_vmem(v) for v in values])


def reduce_to_owner(keep, send):
    owners = lax.axis_size("dp")
    along_x = 4
    along_y = owners // (2 * along_x)
    _, terms, chunk, width = keep.shape

    def move_x(ahead):
        return [
            (d, d - 2 * (d // 2 % along_x) + 2 * ((d // 2 + ahead) % along_x)) for d in range(owners)
        ]

    def move_y(ahead):
        return [(d, (d + ahead * 2 * along_x) % owners) for d in range(owners)]

    came = lax.ppermute(send, "dp", [(d, d ^ 1) for d in range(owners)])
    shape = kept_shape((along_y, terms, chunk, width), BF16)
    own, *others = call_in_vmem(split_x_kernel, (shape,) * along_x, keep, came)
    others = [lax.ppermute(v, "dp", move_x(i + 1)) for i, v in enumerate(others)]
    shape = (terms, chunk, width)
    shapes = (kept_shape(shape, F32),) + (kept_shape(shape, BF16),) * (along_y - 1)
    own, *others = call_in_vmem(functools.partial(split_y_kernel, along_x), shapes, own, *others)
    others = [lax.ppermute(v, "dp", move_y(i + 1)) for i, v in enumerate(others)]
    shapes = (
        jax.ShapeDtypeStruct((terms // 2, chunk, width), F32),
        jax.ShapeDtypeStruct((terms // 2, width, chunk), F32),
    )
    return call_in_vmem(finish_kernel, shapes, own, *others)


def per_device(
    activations, out_grad, w_up, w_down, mod_scale, mod_gate, expert_ids, gate_prob, bucket
):
    features = activations.shape[2]
    experts = w_up.shape[1]
    prepared = prepare(
        activations[0],
        expert_ids[0].T,
        gate_prob[0].T,
        bucket[None, :],
        mod_scale[0],
        mod_gate[0],
        w_up[0],
    )
    grads, outs, pres = run_chain(prepared, out_grad, w_up[0], w_down[0])
    hidden, rows = prepared[6:8]
    keep, send = expert_grads(rows, pres, hidden, outs, lax.axis_size("dp"))
    up_shard, down_shard = reduce_to_owner(keep, send)
    return (grads.reshape(1, -1, features), up_shard[None], down_shard[None])


def solution(mesh):
    return jax.shard_map(
        per_device,
        mesh=mesh,
        in_specs=(
            P("pipe", "dp", None),
            P("dp", None),
            P("pipe", None, None, None),
            P("pipe", None, None, None),
            P("pipe", None, None),
            P("pipe", None, None),
            P("pipe", "dp", None),
            P("pipe", "dp", None),
            P("dp"),
        ),
        out_specs=(P("pipe", "dp", None), P("pipe", None, "dp", None), P("pipe", None, None, "dp")),
        check_vma=False,
    )
```

```python
import functools

import jax
import jax.numpy as jnp
from jax import lax
from jax.experimental import pallas as pl
from jax.experimental.pallas import tpu as pltpu
from jax.sharding import PartitionSpec as P

TOK_MB = 64
CAP = 16
EPSILON = 1e-06
F32 = jnp.float32
BF16 = jnp.bfloat16
VMEM_LIMIT = 24 * 1024 * 1024
STEP_LIMIT = 6 * 1024 * 1024


def in_vmem(value):
    return pltpu.with_memory_space_constraint(value, pltpu.VMEM)


def kept_shape(shape, dtype):
    return pltpu.VMEM(shape, dtype)


def vmem_specs(count):
    return [pl.BlockSpec(memory_space=pltpu.VMEM)] * count


def three_parts(table):
    high = table.astype(BF16)
    rest = table - high.astype(F32)
    middle = rest.astype(BF16)
    low = (rest - middle.astype(F32)).astype(BF16)
    return jnp.concatenate([high, middle, low], axis=0)


def prepare_kernel(
    act_hbm,
    ids_hbm,
    prob_hbm,
    bucket_hbm,
    scale_hbm,
    gate_hbm,
    up_hbm,
    down_hbm,
    top_hbm,
    top_ref,
    take_ref,
    place_ref,
    gate_ref,
    scale_ref,
    normed_ref,
    slope_ref,
    down_ref,
    up_ref,
    _grad_store,
    _outs_store,
    _pres_store,
    _given,
    hidden_ref,
    rows_ref,
    act_ref,
    ids_ref,
    prob_ref,
    bucket_ref,
    scale_table_ref,
    gate_table_ref,
    sems,
):
    moves = [
        (ids_hbm, ids_ref),
        (prob_hbm, prob_ref),
        (bucket_hbm, bucket_ref),
        (scale_hbm, scale_table_ref),
        (gate_hbm, gate_table_ref),
        (act_hbm, act_ref),
        (up_hbm, up_ref),
        (top_hbm, top_ref),
        (down_hbm, down_ref),
    ]
    copies = [
        pltpu.make_async_copy(source, target, sems.at[number])
        for number, (source, target) in enumerate(moves)
    ]
    for copy in copies:
        copy.start()
    for copy in copies[:3]:
        copy.wait()
    tokens = act_ref.shape[0]
    experts = up_ref.shape[0]
    slots = experts * CAP
    features = act_ref.shape[1]
    ids = ids_ref[...]
    prob = prob_ref[...]
    bucket = bucket_ref[...].astype(F32)
    lane = lax.broadcasted_iota(jnp.int32, (1, tokens), 1) % TOK_MB
    slot_no = (lax.broadcasted_iota(jnp.int32, (CAP, tokens), 0) + 1).astype(F32)
    hits = []
    gates = []
    for expert in range(experts):
        chosen = ids == expert
        routed = jnp.max(jnp.where(chosen, 1.0, 0.0), axis=0, keepdims=True)
        token_gate = jnp.sum(jnp.where(chosen, prob, 0.0), axis=0, keepdims=True)
        place = routed
        step = 1
        while step < TOK_MB:
            place = place + jnp.where(lane >= step, pltpu.roll(place, step, 1), 0.0)
            step *= 2
        hit = jnp.where((place == slot_no) & (routed > 0.0), 1.0, 0.0)
        hits.append(hit)
        gates.append(hit * token_gate)
    take = jnp.concatenate(hits, axis=0)
    gates = jnp.concatenate(gates, axis=0)
    buckets = take * bucket
    for copy in copies[3:6]:
        copy.wait()
    tables = three_parts(scale_table_ref[...]), three_parts(gate_table_ref[...])
    entries = scale_table_ref.shape[0]
    wide = lax.broadcasted_iota(jnp.int32, (slots, 2 * TOK_MB), 1)
    eye = jnp.where(
        lax.broadcasted_iota(jnp.int32, (TOK_MB, 2 * TOK_MB), 0)
        == lax.broadcasted_iota(jnp.int32, (TOK_MB, 2 * TOK_MB), 1),
        1.0,
        0.0,
    )
    entry_no = lax.broadcasted_iota(jnp.int32, (slots, 3 * entries), 1) % entries
    for block in range(tokens // TOK_MB):
        pair = slice(block // 2 * 2 * TOK_MB, (block // 2 + 1) * 2 * TOK_MB)
        inside = (wide < TOK_MB) if block % 2 == 0 else (wide >= TOK_MB)
        block_take = jnp.where(inside, take[:, pair], 0.0)
        slot_gate = jnp.sum(jnp.where(inside, gates[:, pair], 0.0), axis=1, keepdims=True)
        slot_bucket = jnp.sum(jnp.where(inside, buckets[:, pair], 0.0), axis=1, keepdims=True)
        raw = jnp.dot(block_take.astype(BF16), act_ref[pair, :], preferred_element_type=F32)
        first = block_take if block % 2 == 0 else pltpu.roll(block_take, TOK_MB, 1)
        take_ref[block] = first.astype(BF16)
        stacked = jnp.concatenate([first, first, eye], axis=0)
        place_ref[block] = jnp.transpose(stacked)[:TOK_MB, :].astype(BF16)
        picked = jnp.where(slot_bucket.astype(jnp.int32) == entry_no, 1.0, 0.0).astype(BF16)
        scale_rows = 1.0 + jnp.dot(picked, tables[0], preferred_element_type=F32)
        gate_rows = jnp.dot(picked, tables[1], preferred_element_type=F32)
        gate_ref[block] = slot_gate * gate_rows
        centred = raw - jnp.mean(raw, axis=-1, keepdims=True)
        inv_std = lax.rsqrt(jnp.mean(centred * centred, axis=-1, keepdims=True) + EPSILON)
        normed = centred * inv_std
        normed_ref[block] = normed
        scale_ref[block] = scale_rows * inv_std
        inputs = (normed * scale_rows).astype(BF16)
        for expert in range(experts):
            rows_ref[expert, block * CAP : (block + 1) * CAP, :] = inputs[
                expert * CAP : (expert + 1) * CAP, :
            ]
    copies[6].wait()
    for expert in range(experts):
        pre_act = jnp.dot(rows_ref[expert], up_ref[expert], preferred_element_type=F32)
        root = 0.7978845608028654
        square = pre_act * pre_act
        bend = jnp.tanh(root * (pre_act + 0.044715 * (square * pre_act)))
        half = 0.5 * (1.0 + bend)
        hidden_ref[expert] = (pre_act * half).astype(BF16)
        slope = half + 0.5 * pre_act * (1.0 - bend * bend) * (root * (1.0 + 0.134145 * square))
        slope_ref[expert] = slope.reshape(slope_ref.shape[1:])
    for copy in copies[7:]:
        copy.wait()


def prepare(act, ids, prob, bucket, scale_table, gate_table, up_mats, down_mats, out_grad):
    tokens, features = act.shape
    experts, _, width = up_mats.shape
    blocks = tokens // TOK_MB
    slots = experts * CAP
    top = out_grad.reshape(blocks, TOK_MB, features)
    values = (act, ids, prob, bucket, scale_table, gate_table, up_mats, down_mats, top)
    out_shape = (
        kept_shape(top.shape, BF16),
        kept_shape((blocks, slots, 2 * TOK_MB), BF16),
        kept_shape((blocks, TOK_MB, 2 * slots + TOK_MB), BF16),
        kept_shape((blocks, slots, features), F32),
        kept_shape((blocks, slots, features), F32),
        kept_shape((blocks, slots, features), F32),
        kept_shape((experts, blocks, CAP, width), F32),
        kept_shape(down_mats.shape, BF16),
        kept_shape(up_mats.shape, BF16),
        kept_shape((blocks, TOK_MB, features), BF16),
        kept_shape((experts, blocks, CAP, features), BF16),
        kept_shape((experts, blocks, CAP, width), BF16),
        kept_shape((TOK_MB, features), BF16),
        kept_shape((experts, blocks * CAP, width), BF16),
        kept_shape((experts, blocks * CAP, features), BF16),
    )
    return pl.pallas_call(
        prepare_kernel,
        out_shape=out_shape,
        in_specs=[pl.BlockSpec(memory_space=pltpu.HBM)] * len(values),
        out_specs=tuple(vmem_specs(len(out_shape))),
        scratch_shapes=[pltpu.VMEM(v.shape, v.dtype) for v in values[:6]]
        + [pltpu.SemaphoreType.DMA((len(values),))],
        compiler_params=pltpu.CompilerParams(vmem_limit_bytes=VMEM_LIMIT),
    )(*[pltpu.with_memory_space_constraint(v, pltpu.HBM) for v in values])


def step_kernel(
    cycle,
    parity,
    given_ref,
    top_ref,
    take_ref,
    place_ref,
    gate_ref,
    scale_ref,
    normed_ref,
    slope_ref,
    down_ref,
    up_ref,
    _grad_in,
    _outs_in,
    _pres_in,
    grad_ref,
    outs_ref,
    pres_ref,
    *sent_refs,
):
    experts = down_ref.shape[0]
    blocks = take_ref.shape[0]
    depth = lax.axis_size("pipe") - 1 - lax.axis_index("pipe")
    block = block_of(cycle, depth)

    @pl.when((depth % 2 == parity) & (block >= 0) & (block < blocks))
    def _():
        grad_out = jnp.where(depth == 0, top_ref[block], given_ref[...])
        gathered = jnp.dot(take_ref[block][:, :TOK_MB], grad_out, preferred_element_type=F32)
        outs = (gate_ref[block] * gathered).astype(BF16)
        back = []
        for expert in range(experts):
            rows = slice(expert * CAP, (expert + 1) * CAP)
            outs_ref[expert, block] = outs[rows, :]
            hid_grad = turned_dot(outs[rows, :], down_ref[expert])
            pres = (hid_grad * slope_ref[expert, block]).astype(BF16)
            pres_ref[expert, block] = pres
            back.append(turned_dot(pres, up_ref[expert]))
        varied = jnp.concatenate(back, axis=0) * scale_ref[block]
        normed = normed_ref[block]
        lifted = (
            varied
            - jnp.mean(varied, axis=-1, keepdims=True)
            - normed * jnp.mean(varied * normed, axis=-1, keepdims=True)
        )
        high = lifted.astype(BF16)
        low = (lifted - high.astype(F32)).astype(BF16)
        parts = jnp.concatenate([high, low, grad_out], axis=0)
        grad_in = jnp.dot(place_ref[block], parts, preferred_element_type=F32).astype(BF16)
        for sent_ref in sent_refs:
            sent_ref[...] = grad_in
        grad_ref[block] = grad_in


def turned_dot(left, right):
    return lax.dot_general(left, right, (((1,), (1,)), ((), ())), preferred_element_type=F32)


def run_step(cycle, parity, given, fixed, stores, sends):
    out_shape = stores + (given,) * sends
    count = 1 + len(fixed)
    return pl.pallas_call(
        functools.partial(step_kernel, cycle, parity),
        out_shape=tuple(kept_shape(v.shape, v.dtype) for v in out_shape),
        in_specs=vmem_specs(count + len(stores)),
        out_specs=tuple(vmem_specs(len(out_shape))),
        input_output_aliases={count + i: i for i in range(len(stores))},
        compiler_params=pltpu.CompilerParams(vmem_limit_bytes=STEP_LIMIT),
    )(in_vmem(given), *[in_vmem(v) for v in fixed], *[in_vmem(v) for v in stores])


def block_of(cycle, depth):
    return cycle - depth // 2 * 3 - depth % 2


def run_chain(prepared):
    fixed, stores, given = prepared[:9], prepared[9:12], prepared[12]
    blocks = fixed[0].shape[0]
    sections = lax.axis_size("pipe")
    waiting = {0: [given, given], 1: [given]}
    cycles = sections // 2 * 3 + blocks
    for cycle in range(cycles):
        for parity in (0, 1):
            senders = [
                depth
                for depth in range(parity, sections, 2)
                if 0 <= block_of(cycle, depth) < blocks
            ]
            came = waiting[parity].pop(0)
            if not senders:
                waiting[1 - parity].append(came)
                continue
            pairs = [(sections - 1 - d, sections - 2 - d) for d in senders if d < sections - 1]
            results = run_step(cycle, parity, came, fixed, stores, len(pairs) > 0)
            stores = results[:3]
            if pairs:
                came = lax.ppermute(results[3], "pipe", pairs)
            waiting[1 - parity].append(came)
    return tuple(stores)


def grads_kernel(rows_ref, pres_ref, hidden_ref, outs_ref, keep_ref, send_ref):
    experts, blocks, cap, features = outs_ref.shape
    chunk = keep_ref.shape[2]
    tile = 256
    core = lax.axis_index("dp") % 2
    terms = []
    for e in range(experts):
        terms.append((rows_ref[e], pres_ref[e].reshape(blocks * cap, -1)))
    for e in range(experts):
        terms.append((outs_ref[e].reshape(blocks * cap, features), hidden_ref[e]))
    for number, (left, right) in enumerate(terms):
        for start in range(0, features, tile):
            part = lax.dot_general(
                left[:, start : start + tile],
                right,
                (((0,), (0,)), ((), ())),
                preferred_element_type=F32,
            ).astype(BF16)
            for pair in range(tile // (2 * chunk)):
                place = start // (2 * chunk) + pair
                low = part[2 * pair * chunk : (2 * pair + 1) * chunk]
                high = part[(2 * pair + 1) * chunk : (2 * pair + 2) * chunk]
                keep_ref[place, number] = jnp.where(core == 0, low, high)
                send_ref[place, number] = jnp.where(core == 0, high, low)


def expert_grads(rows, pres, hidden, outs, owners):
    experts, _, features = rows.shape
    width = pres.shape[-1]
    shape = (owners // 2, 2 * experts, features // owners, width)
    return pl.pallas_call(
        grads_kernel,
        out_shape=(kept_shape(shape, BF16),) * 2,
        in_specs=vmem_specs(4),
        out_specs=tuple(vmem_specs(2)),
        compiler_params=pltpu.CompilerParams(vmem_limit_bytes=VMEM_LIMIT),
    )(in_vmem(rows), in_vmem(pres), in_vmem(hidden), in_vmem(outs))


def split_x_kernel(along_x, keep_ref, came_ref, own_ref, right_ref, left_ref, next_ref, past_ref):
    my_x = lax.axis_index("dp") // 2 % along_x
    half = right_ref.shape[2]
    for row in range(own_ref.shape[0]):
        parts = []
        for ahead in range(along_x):
            place = row * along_x + (my_x + ahead) % along_x
            part = keep_ref[place].astype(F32) + came_ref[place].astype(F32)
            parts.append(part.astype(BF16))
        own_ref[row] = parts[0]
        right_ref[0, row] = parts[2][:half]
        right_ref[1, row] = parts[1][half:]
        left_ref[0, row] = parts[2][half:]
        left_ref[1, row] = parts[3][:half]
        next_ref[row] = parts[1][:half]
        past_ref[row] = parts[3][half:]


def relay_kernel(next_ref, past_ref, from_left_ref, from_right_ref, right_ref, left_ref):
    right_ref[...] = (next_ref[...].astype(F32) + from_left_ref[0].astype(F32)).astype(BF16)
    left_ref[...] = (past_ref[...].astype(F32) + from_right_ref[0].astype(F32)).astype(BF16)


def split_y_kernel(own_ref, first_left, first_right, left_ref, right_ref, *part_refs):
    along_y = len(part_refs)
    half = left_ref.shape[1]
    my_y = lax.axis_index("dp") // (lax.axis_size("dp") // along_y)
    for ahead, part_ref in enumerate(part_refs):
        row = (my_y + ahead) % along_y
        low = left_ref[row].astype(F32) + first_right[1, row].astype(F32)
        high = right_ref[row].astype(F32) + first_left[1, row].astype(F32)
        total = own_ref[row].astype(F32)
        part_ref[:half] = (total[:half] + low).astype(part_ref.dtype)
        part_ref[half:] = (total[half:] + high).astype(part_ref.dtype)


def finish_kernel(own_ref, *refs):
    came_refs, (up_ref, down_ref) = refs[:-2], refs[-2:]
    experts = up_ref.shape[0]
    for number in range(2 * experts):
        total = own_ref[number]
        for came_ref in came_refs:
            total = total + came_ref[number].astype(F32)
        if number < experts:
            up_ref[number] = total
        else:
            down_ref[number - experts] = jnp.transpose(total)


def call_in_vmem(kernel, out_shape, *values):
    return pl.pallas_call(
        kernel,
        out_shape=out_shape,
        in_specs=vmem_specs(len(values)),
        out_specs=tuple(vmem_specs(len(out_shape))),
        compiler_params=pltpu.CompilerParams(vmem_limit_bytes=VMEM_LIMIT),
    )(*[in_vmem(v) for v in values])


def reduce_to_owner(keep, send):
    owners = lax.axis_size("dp")
    along_x = 4
    along_y = owners // (2 * along_x)
    _, terms, chunk, width = keep.shape

    def move_x(ahead):
        return [
            (d, d - 2 * (d // 2 % along_x) + 2 * ((d // 2 + ahead) % along_x)) for d in range(owners)
        ]

    def move_y(ahead):
        return [(d, (d + ahead * 2 * along_x) % owners) for d in range(owners)]

    came = lax.ppermute(send, "dp", [(d, d ^ 1) for d in range(owners)])
    half = terms // 2
    whole = kept_shape((along_y, terms, chunk, width), BF16)
    double = kept_shape((2, along_y, half, chunk, width), BF16)
    single = kept_shape((along_y, half, chunk, width), BF16)
    own, right, left, following, past = call_in_vmem(
        functools.partial(split_x_kernel, along_x),
        (whole, double, double, single, single),
        keep,
        came,
    )
    first_left = lax.ppermute(right, "dp", move_x(1))
    first_right = lax.ppermute(left, "dp", move_x(-1))
    right, left = call_in_vmem(
        relay_kernel, (single, single), following, past, first_left, first_right
    )
    last_left = lax.ppermute(right, "dp", move_x(1))
    last_right = lax.ppermute(left, "dp", move_x(-1))
    shape = (terms, chunk, width)
    shapes = (kept_shape(shape, F32),) + (kept_shape(shape, BF16),) * (along_y - 1)
    own, *others = call_in_vmem(
        split_y_kernel, shapes, own, first_left, first_right, last_left, last_right
    )
    others = [lax.ppermute(v, "dp", move_y(i + 1)) for i, v in enumerate(others)]
    shapes = (
        jax.ShapeDtypeStruct((terms // 2, chunk, width), F32),
        jax.ShapeDtypeStruct((terms // 2, width, chunk), F32),
    )
    return call_in_vmem(finish_kernel, shapes, own, *others)


def per_device(
    activations, out_grad, w_up, w_down, mod_scale, mod_gate, expert_ids, gate_prob, bucket
):
    features = activations.shape[2]
    prepared = prepare(
        activations[0],
        expert_ids[0].T,
        gate_prob[0].T,
        bucket[None, :],
        mod_scale[0],
        mod_gate[0],
        w_up[0],
        w_down[0],
        out_grad,
    )
    grads, outs, pres = run_chain(prepared)
    hidden, rows = prepared[13:]
    keep, send = expert_grads(rows, pres, hidden, outs, lax.axis_size("dp"))
    up_shard, down_shard = reduce_to_owner(keep, send)
    return (grads.reshape(1, -1, features), up_shard[None], down_shard[None])


def solution(mesh):
    return jax.shard_map(
        per_device,
        mesh=mesh,
        in_specs=(
            P("pipe", "dp", None),
            P("dp", None),
            P("pipe", None, None, None),
            P("pipe", None, None, None),
            P("pipe", None, None),
            P("pipe", None, None),
            P("pipe", "dp", None),
            P("pipe", "dp", None),
            P("dp"),
        ),
        out_specs=(P("pipe", "dp", None), P("pipe", None, "dp", None), P("pipe", None, None, "dp")),
        check_vma=False,
    )
```

```python
import functools

import jax
import jax.numpy as jnp
from jax import lax
from jax.experimental import pallas as pl
from jax.experimental.pallas import tpu as pltpu
from jax.sharding import PartitionSpec as P

TOK_MB = 64
CAP = 16
EPSILON = 1e-06
F32 = jnp.float32
BF16 = jnp.bfloat16
VMEM_LIMIT = 24 * 1024 * 1024
STEP_LIMIT = 6 * 1024 * 1024


def in_vmem(value):
    return pltpu.with_memory_space_constraint(value, pltpu.VMEM)


def kept_shape(shape, dtype):
    return pltpu.VMEM(shape, dtype)


def vmem_specs(count):
    return [pl.BlockSpec(memory_space=pltpu.VMEM)] * count


def three_parts(table):
    high = table.astype(BF16)
    rest = table - high.astype(F32)
    middle = rest.astype(BF16)
    low = (rest - middle.astype(F32)).astype(BF16)
    return jnp.concatenate([high, middle, low], axis=0)


def prepare_kernel(
    act_hbm,
    ids_hbm,
    prob_hbm,
    bucket_hbm,
    scale_hbm,
    gate_hbm,
    up_hbm,
    down_hbm,
    top_hbm,
    top_ref,
    take_ref,
    place_ref,
    gate_ref,
    scale_ref,
    normed_ref,
    slope_ref,
    down_ref,
    up_ref,
    _grad_store,
    _outs_store,
    _pres_store,
    _given,
    hidden_ref,
    rows_ref,
    act_ref,
    ids_ref,
    prob_ref,
    bucket_ref,
    scale_table_ref,
    gate_table_ref,
    sems,
):
    moves = [
        (ids_hbm, ids_ref),
        (prob_hbm, prob_ref),
        (bucket_hbm, bucket_ref),
        (scale_hbm, scale_table_ref),
        (gate_hbm, gate_table_ref),
        (act_hbm, act_ref),
        (up_hbm, up_ref),
        (top_hbm, top_ref),
        (down_hbm, down_ref),
    ]
    copies = [
        pltpu.make_async_copy(source, target, sems.at[number])
        for number, (source, target) in enumerate(moves)
    ]
    for copy in copies:
        copy.start()
    for copy in copies[:3]:
        copy.wait()
    tokens = act_ref.shape[0]
    experts = up_ref.shape[0]
    slots = experts * CAP
    features = act_ref.shape[1]
    ids = ids_ref[...]
    prob = prob_ref[...]
    bucket = bucket_ref[...].astype(F32)
    lane = lax.broadcasted_iota(jnp.int32, (1, tokens), 1) % TOK_MB
    slot_no = (lax.broadcasted_iota(jnp.int32, (CAP, tokens), 0) + 1).astype(F32)
    hits = []
    gates = []
    for expert in range(experts):
        chosen = ids == expert
        routed = jnp.max(jnp.where(chosen, 1.0, 0.0), axis=0, keepdims=True)
        token_gate = jnp.sum(jnp.where(chosen, prob, 0.0), axis=0, keepdims=True)
        place = routed
        step = 1
        while step < TOK_MB:
            place = place + jnp.where(lane >= step, pltpu.roll(place, step, 1), 0.0)
            step *= 2
        hit = jnp.where((place == slot_no) & (routed > 0.0), 1.0, 0.0)
        hits.append(hit)
        gates.append(hit * token_gate)
    take = jnp.concatenate(hits, axis=0)
    gates = jnp.concatenate(gates, axis=0)
    buckets = take * bucket
    for copy in copies[3:6]:
        copy.wait()
    tables = three_parts(scale_table_ref[...]), three_parts(gate_table_ref[...])
    entries = scale_table_ref.shape[0]
    wide = lax.broadcasted_iota(jnp.int32, (slots, 2 * TOK_MB), 1)
    eye = jnp.where(
        lax.broadcasted_iota(jnp.int32, (TOK_MB, 2 * TOK_MB), 0)
        == lax.broadcasted_iota(jnp.int32, (TOK_MB, 2 * TOK_MB), 1),
        1.0,
        0.0,
    )
    entry_no = lax.broadcasted_iota(jnp.int32, (slots, 3 * entries), 1) % entries
    for block in range(tokens // TOK_MB):
        pair = slice(block // 2 * 2 * TOK_MB, (block // 2 + 1) * 2 * TOK_MB)
        inside = (wide < TOK_MB) if block % 2 == 0 else (wide >= TOK_MB)
        block_take = jnp.where(inside, take[:, pair], 0.0)
        slot_gate = jnp.sum(jnp.where(inside, gates[:, pair], 0.0), axis=1, keepdims=True)
        slot_bucket = jnp.sum(jnp.where(inside, buckets[:, pair], 0.0), axis=1, keepdims=True)
        raw = jnp.dot(block_take.astype(BF16), act_ref[pair, :], preferred_element_type=F32)
        first = block_take if block % 2 == 0 else pltpu.roll(block_take, TOK_MB, 1)
        take_ref[block] = first.astype(BF16)
        stacked = jnp.concatenate([first, first, eye], axis=0)
        place_ref[block] = jnp.transpose(stacked)[:TOK_MB, :].astype(BF16)
        picked = jnp.where(slot_bucket.astype(jnp.int32) == entry_no, 1.0, 0.0).astype(BF16)
        scale_rows = 1.0 + jnp.dot(picked, tables[0], preferred_element_type=F32)
        gate_rows = jnp.dot(picked, tables[1], preferred_element_type=F32)
        gate_ref[block] = slot_gate * gate_rows
        centred = raw - jnp.mean(raw, axis=-1, keepdims=True)
        inv_std = lax.rsqrt(jnp.mean(centred * centred, axis=-1, keepdims=True) + EPSILON)
        normed = centred * inv_std
        normed_ref[block] = normed
        scale_ref[block] = scale_rows * inv_std
        inputs = (normed * scale_rows).astype(BF16)
        for expert in range(experts):
            rows_ref[expert, block * CAP : (block + 1) * CAP, :] = inputs[
                expert * CAP : (expert + 1) * CAP, :
            ]
    copies[6].wait()
    for expert in range(experts):
        pre_act = jnp.dot(rows_ref[expert], up_ref[expert], preferred_element_type=F32)
        root = 0.7978845608028654
        square = pre_act * pre_act
        bend = jnp.tanh(root * (pre_act + 0.044715 * (square * pre_act)))
        half = 0.5 * (1.0 + bend)
        hidden_ref[expert] = (pre_act * half).astype(BF16)
        slope = half + 0.5 * pre_act * (1.0 - bend * bend) * (root * (1.0 + 0.134145 * square))
        slope_ref[expert] = slope.reshape(slope_ref.shape[1:])
    for copy in copies[7:]:
        copy.wait()


def prepare(act, ids, prob, bucket, scale_table, gate_table, up_mats, down_mats, out_grad):
    tokens, features = act.shape
    experts, _, width = up_mats.shape
    blocks = tokens // TOK_MB
    slots = experts * CAP
    top = out_grad.reshape(blocks, TOK_MB, features)
    values = (act, ids, prob, bucket, scale_table, gate_table, up_mats, down_mats, top)
    out_shape = (
        kept_shape(top.shape, BF16),
        kept_shape((blocks, slots, 2 * TOK_MB), BF16),
        kept_shape((blocks, TOK_MB, 2 * slots + TOK_MB), BF16),
        kept_shape((blocks, slots, features), F32),
        kept_shape((blocks, slots, features), F32),
        kept_shape((blocks, slots, features), F32),
        kept_shape((experts, blocks, CAP, width), F32),
        kept_shape(down_mats.shape, BF16),
        kept_shape(up_mats.shape, BF16),
        kept_shape((blocks, TOK_MB, features), BF16),
        kept_shape((experts, blocks, CAP, features), BF16),
        kept_shape((experts, blocks, CAP, width), BF16),
        kept_shape((TOK_MB, features), BF16),
        kept_shape((experts, blocks * CAP, width), BF16),
        kept_shape((experts, blocks * CAP, features), BF16),
    )
    return pl.pallas_call(
        prepare_kernel,
        out_shape=out_shape,
        in_specs=[pl.BlockSpec(memory_space=pltpu.HBM)] * len(values),
        out_specs=tuple(vmem_specs(len(out_shape))),
        scratch_shapes=[pltpu.VMEM(v.shape, v.dtype) for v in values[:6]]
        + [pltpu.SemaphoreType.DMA((len(values),))],
        compiler_params=pltpu.CompilerParams(vmem_limit_bytes=VMEM_LIMIT),
    )(*[pltpu.with_memory_space_constraint(v, pltpu.HBM) for v in values])


def step_kernel(
    cycle,
    parity,
    given_ref,
    top_ref,
    take_ref,
    place_ref,
    gate_ref,
    scale_ref,
    normed_ref,
    slope_ref,
    down_ref,
    up_ref,
    _grad_in,
    _outs_in,
    _pres_in,
    grad_ref,
    outs_ref,
    pres_ref,
    *sent_refs,
):
    experts = down_ref.shape[0]
    blocks = take_ref.shape[0]
    depth = lax.axis_size("pipe") - 1 - lax.axis_index("pipe")
    block = block_of(cycle, depth)

    @pl.when((depth % 2 == parity) & (block >= 0) & (block < blocks))
    def _():
        grad_out = jnp.where(depth == 0, top_ref[block], given_ref[...])
        gathered = jnp.dot(take_ref[block][:, :TOK_MB], grad_out, preferred_element_type=F32)
        outs = (gate_ref[block] * gathered).astype(BF16)
        back = []
        for expert in range(experts):
            rows = slice(expert * CAP, (expert + 1) * CAP)
            outs_ref[expert, block] = outs[rows, :]
            hid_grad = turned_dot(outs[rows, :], down_ref[expert])
            pres = (hid_grad * slope_ref[expert, block]).astype(BF16)
            pres_ref[expert, block] = pres
            back.append(turned_dot(pres, up_ref[expert]))
        varied = jnp.concatenate(back, axis=0) * scale_ref[block]
        normed = normed_ref[block]
        lifted = (
            varied
            - jnp.mean(varied, axis=-1, keepdims=True)
            - normed * jnp.mean(varied * normed, axis=-1, keepdims=True)
        )
        high = lifted.astype(BF16)
        low = (lifted - high.astype(F32)).astype(BF16)
        parts = jnp.concatenate([high, low, grad_out], axis=0)
        grad_in = jnp.dot(place_ref[block], parts, preferred_element_type=F32).astype(BF16)
        for sent_ref in sent_refs:
            sent_ref[...] = grad_in
        grad_ref[block] = grad_in


def turned_dot(left, right):
    return lax.dot_general(left, right, (((1,), (1,)), ((), ())), preferred_element_type=F32)


def run_step(cycle, parity, given, fixed, stores, sends):
    out_shape = stores + (given,) * sends
    count = 1 + len(fixed)
    return pl.pallas_call(
        functools.partial(step_kernel, cycle, parity),
        out_shape=tuple(kept_shape(v.shape, v.dtype) for v in out_shape),
        in_specs=vmem_specs(count + len(stores)),
        out_specs=tuple(vmem_specs(len(out_shape))),
        input_output_aliases={count + i: i for i in range(len(stores))},
        compiler_params=pltpu.CompilerParams(vmem_limit_bytes=STEP_LIMIT),
    )(in_vmem(given), *[in_vmem(v) for v in fixed], *[in_vmem(v) for v in stores])


def block_of(cycle, depth):
    return cycle - depth // 2 * 3 - depth % 2


def run_chain(prepared):
    fixed, stores, given = prepared[:9], prepared[9:12], prepared[12]
    blocks = fixed[0].shape[0]
    sections = lax.axis_size("pipe")
    waiting = {0: [given, given], 1: [given]}
    cycles = sections // 2 * 3 + blocks
    for cycle in range(cycles):
        for parity in (0, 1):
            senders = [
                depth
                for depth in range(parity, sections, 2)
                if 0 <= block_of(cycle, depth) < blocks
            ]
            came = waiting[parity].pop(0)
            if not senders:
                waiting[1 - parity].append(came)
                continue
            window = 8
            first = senders[0] // window * window
            last = (senders[-1] // window + 1) * window
            depths = range(first + parity, min(last, sections - 1), 2)
            pairs = [(sections - 1 - d, sections - 2 - d) for d in depths]
            if senders[0] >= sections - 1:
                pairs = []
            results = run_step(cycle, parity, came, fixed, stores, len(pairs) > 0)
            stores = results[:3]
            if pairs:
                came = lax.ppermute(results[3], "pipe", pairs)
            waiting[1 - parity].append(came)
    return tuple(stores)


def grads_kernel(rows_ref, pres_ref, hidden_ref, outs_ref, keep_ref, send_ref):
    experts, blocks, cap, features = outs_ref.shape
    chunk = keep_ref.shape[2]
    tile = 256
    core = lax.axis_index("dp") % 2
    terms = []
    for e in range(experts):
        terms.append((rows_ref[e], pres_ref[e].reshape(blocks * cap, -1)))
    for e in range(experts):
        terms.append((outs_ref[e].reshape(blocks * cap, features), hidden_ref[e]))
    for number, (left, right) in enumerate(terms):
        for start in range(0, features, tile):
            part = lax.dot_general(
                left[:, start : start + tile],
                right,
                (((0,), (0,)), ((), ())),
                preferred_element_type=F32,
            ).astype(BF16)
            for pair in range(tile // (2 * chunk)):
                place = start // (2 * chunk) + pair
                low = part[2 * pair * chunk : (2 * pair + 1) * chunk]
                high = part[(2 * pair + 1) * chunk : (2 * pair + 2) * chunk]
                keep_ref[place, number] = jnp.where(core == 0, low, high)
                send_ref[place, number] = jnp.where(core == 0, high, low)


def expert_grads(rows, pres, hidden, outs, owners):
    experts, _, features = rows.shape
    width = pres.shape[-1]
    shape = (owners // 2, 2 * experts, features // owners, width)
    return pl.pallas_call(
        grads_kernel,
        out_shape=(kept_shape(shape, BF16),) * 2,
        in_specs=vmem_specs(4),
        out_specs=tuple(vmem_specs(2)),
        compiler_params=pltpu.CompilerParams(vmem_limit_bytes=VMEM_LIMIT),
    )(in_vmem(rows), in_vmem(pres), in_vmem(hidden), in_vmem(outs))


def split_x_kernel(along_x, keep_ref, came_ref, own_ref, right_ref, left_ref, next_ref, past_ref):
    my_x = lax.axis_index("dp") // 2 % along_x
    half = right_ref.shape[2]
    for row in range(own_ref.shape[0]):
        parts = []
        for ahead in range(along_x):
            place = row * along_x + (my_x + ahead) % along_x
            part = keep_ref[place].astype(F32) + came_ref[place].astype(F32)
            parts.append(part.astype(BF16))
        own_ref[row] = parts[0]
        right_ref[0, row] = parts[2][:half]
        right_ref[1, row] = parts[1][half:]
        left_ref[0, row] = parts[2][half:]
        left_ref[1, row] = parts[3][:half]
        next_ref[row] = parts[1][:half]
        past_ref[row] = parts[3][half:]


def relay_kernel(next_ref, past_ref, from_left_ref, from_right_ref, right_ref, left_ref):
    right_ref[...] = (next_ref[...].astype(F32) + from_left_ref[0].astype(F32)).astype(BF16)
    left_ref[...] = (past_ref[...].astype(F32) + from_right_ref[0].astype(F32)).astype(BF16)


def split_y_kernel(own_ref, first_left, first_right, left_ref, right_ref, *part_refs):
    along_y = len(part_refs)
    half = left_ref.shape[1]
    my_y = lax.axis_index("dp") // (lax.axis_size("dp") // along_y)
    for ahead, part_ref in enumerate(part_refs):
        row = (my_y + ahead) % along_y
        low = left_ref[row].astype(F32) + first_right[1, row].astype(F32)
        high = right_ref[row].astype(F32) + first_left[1, row].astype(F32)
        total = own_ref[row].astype(F32)
        part_ref[:half] = (total[:half] + low).astype(part_ref.dtype)
        part_ref[half:] = (total[half:] + high).astype(part_ref.dtype)


def finish_kernel(own_ref, *refs):
    came_refs, (up_ref, down_ref) = refs[:-2], refs[-2:]
    experts = up_ref.shape[0]
    for number in range(2 * experts):
        total = own_ref[number]
        for came_ref in came_refs:
            total = total + came_ref[number].astype(F32)
        if number < experts:
            up_ref[number] = total
        else:
            down_ref[number - experts] = jnp.transpose(total)


def call_in_vmem(kernel, out_shape, *values):
    return pl.pallas_call(
        kernel,
        out_shape=out_shape,
        in_specs=vmem_specs(len(values)),
        out_specs=tuple(vmem_specs(len(out_shape))),
        compiler_params=pltpu.CompilerParams(vmem_limit_bytes=VMEM_LIMIT),
    )(*[in_vmem(v) for v in values])


def reduce_to_owner(keep, send):
    owners = lax.axis_size("dp")
    along_x = 4
    along_y = owners // (2 * along_x)
    _, terms, chunk, width = keep.shape

    def move_x(ahead):
        return [
            (d, d - 2 * (d // 2 % along_x) + 2 * ((d // 2 + ahead) % along_x)) for d in range(owners)
        ]

    def move_y(ahead):
        return [(d, (d + ahead * 2 * along_x) % owners) for d in range(owners)]

    came = lax.ppermute(send, "dp", [(d, d ^ 1) for d in range(owners)])
    half = terms // 2
    whole = kept_shape((along_y, terms, chunk, width), BF16)
    double = kept_shape((2, along_y, half, chunk, width), BF16)
    single = kept_shape((along_y, half, chunk, width), BF16)
    own, right, left, following, past = call_in_vmem(
        functools.partial(split_x_kernel, along_x),
        (whole, double, double, single, single),
        keep,
        came,
    )
    first_left = lax.ppermute(right, "dp", move_x(1))
    first_right = lax.ppermute(left, "dp", move_x(-1))
    right, left = call_in_vmem(
        relay_kernel, (single, single), following, past, first_left, first_right
    )
    last_left = lax.ppermute(right, "dp", move_x(1))
    last_right = lax.ppermute(left, "dp", move_x(-1))
    shape = (terms, chunk, width)
    shapes = (kept_shape(shape, F32),) + (kept_shape(shape, BF16),) * (along_y - 1)
    own, *others = call_in_vmem(
        split_y_kernel, shapes, own, first_left, first_right, last_left, last_right
    )
    others = [lax.ppermute(v, "dp", move_y(i + 1)) for i, v in enumerate(others)]
    shapes = (
        jax.ShapeDtypeStruct((terms // 2, chunk, width), F32),
        jax.ShapeDtypeStruct((terms // 2, width, chunk), F32),
    )
    return call_in_vmem(finish_kernel, shapes, own, *others)


def per_device(
    activations, out_grad, w_up, w_down, mod_scale, mod_gate, expert_ids, gate_prob, bucket
):
    features = activations.shape[2]
    prepared = prepare(
        activations[0],
        expert_ids[0].T,
        gate_prob[0].T,
        bucket[None, :],
        mod_scale[0],
        mod_gate[0],
        w_up[0],
        w_down[0],
        out_grad,
    )
    grads, outs, pres = run_chain(prepared)
    hidden, rows = prepared[13:]
    keep, send = expert_grads(rows, pres, hidden, outs, lax.axis_size("dp"))
    up_shard, down_shard = reduce_to_owner(keep, send)
    return (grads.reshape(1, -1, features), up_shard[None], down_shard[None])


def solution(mesh):
    return jax.shard_map(
        per_device,
        mesh=mesh,
        in_specs=(
            P("pipe", "dp", None),
            P("dp", None),
            P("pipe", None, None, None),
            P("pipe", None, None, None),
            P("pipe", None, None),
            P("pipe", None, None),
            P("pipe", "dp", None),
            P("pipe", "dp", None),
            P("dp"),
        ),
        out_specs=(P("pipe", "dp", None), P("pipe", None, "dp", None), P("pipe", None, None, "dp")),
        check_vma=False,
    )
```

```python
import functools

import jax
import jax.numpy as jnp
from jax import lax
from jax.experimental import pallas as pl
from jax.experimental.pallas import tpu as pltpu
from jax.sharding import PartitionSpec as P

TOK_MB = 64
CAP = 16
EPSILON = 1e-06
F32 = jnp.float32
BF16 = jnp.bfloat16
VMEM_LIMIT = 24 * 1024 * 1024
STEP_LIMIT = 6 * 1024 * 1024


def in_vmem(value):
    return pltpu.with_memory_space_constraint(value, pltpu.VMEM)


def kept_shape(shape, dtype):
    return pltpu.VMEM(shape, dtype)


def vmem_specs(count):
    return [pl.BlockSpec(memory_space=pltpu.VMEM)] * count


def three_parts(table):
    high = table.astype(BF16)
    rest = table - high.astype(F32)
    middle = rest.astype(BF16)
    low = (rest - middle.astype(F32)).astype(BF16)
    return jnp.concatenate([high, middle, low], axis=0)


def prepare_kernel(
    act_hbm,
    ids_hbm,
    prob_hbm,
    bucket_hbm,
    scale_hbm,
    gate_hbm,
    up_hbm,
    down_hbm,
    top_hbm,
    top_ref,
    take_ref,
    place_ref,
    gate_ref,
    scale_ref,
    normed_ref,
    slope_ref,
    down_ref,
    up_ref,
    _grad_store,
    _outs_store,
    _pres_store,
    _given,
    hidden_ref,
    rows_ref,
    act_ref,
    ids_ref,
    prob_ref,
    bucket_ref,
    scale_table_ref,
    gate_table_ref,
    sems,
):
    moves = [
        (ids_hbm, ids_ref),
        (prob_hbm, prob_ref),
        (bucket_hbm, bucket_ref),
        (scale_hbm, scale_table_ref),
        (gate_hbm, gate_table_ref),
        (act_hbm, act_ref),
        (up_hbm, up_ref),
        (top_hbm, top_ref),
        (down_hbm, down_ref),
    ]
    copies = [
        pltpu.make_async_copy(source, target, sems.at[number])
        for number, (source, target) in enumerate(moves)
    ]
    for copy in copies:
        copy.start()
    for copy in copies[:3]:
        copy.wait()
    tokens = act_ref.shape[0]
    experts = up_ref.shape[0]
    slots = experts * CAP
    features = act_ref.shape[1]
    ids = ids_ref[...]
    prob = prob_ref[...]
    bucket = bucket_ref[...].astype(F32)
    lane = lax.broadcasted_iota(jnp.int32, (1, tokens), 1) % TOK_MB
    slot_no = (lax.broadcasted_iota(jnp.int32, (CAP, tokens), 0) + 1).astype(F32)
    hits = []
    gates = []
    for expert in range(experts):
        chosen = ids == expert
        routed = jnp.max(jnp.where(chosen, 1.0, 0.0), axis=0, keepdims=True)
        token_gate = jnp.sum(jnp.where(chosen, prob, 0.0), axis=0, keepdims=True)
        place = routed
        step = 1
        while step < TOK_MB:
            place = place + jnp.where(lane >= step, pltpu.roll(place, step, 1), 0.0)
            step *= 2
        hit = jnp.where((place == slot_no) & (routed > 0.0), 1.0, 0.0)
        hits.append(hit)
        gates.append(hit * token_gate)
    take = jnp.concatenate(hits, axis=0)
    gates = jnp.concatenate(gates, axis=0)
    buckets = take * bucket
    for copy in copies[3:6]:
        copy.wait()
    tables = three_parts(scale_table_ref[...]), three_parts(gate_table_ref[...])
    entries = scale_table_ref.shape[0]
    wide = lax.broadcasted_iota(jnp.int32, (slots, 2 * TOK_MB), 1)
    eye = jnp.where(
        lax.broadcasted_iota(jnp.int32, (TOK_MB, 2 * TOK_MB), 0)
        == lax.broadcasted_iota(jnp.int32, (TOK_MB, 2 * TOK_MB), 1),
        1.0,
        0.0,
    )
    entry_no = lax.broadcasted_iota(jnp.int32, (slots, 3 * entries), 1) % entries
    for block in range(tokens // TOK_MB):
        pair = slice(block // 2 * 2 * TOK_MB, (block // 2 + 1) * 2 * TOK_MB)
        inside = (wide < TOK_MB) if block % 2 == 0 else (wide >= TOK_MB)
        block_take = jnp.where(inside, take[:, pair], 0.0)
        slot_gate = jnp.sum(jnp.where(inside, gates[:, pair], 0.0), axis=1, keepdims=True)
        slot_bucket = jnp.sum(jnp.where(inside, buckets[:, pair], 0.0), axis=1, keepdims=True)
        raw = jnp.dot(block_take.astype(BF16), act_ref[pair, :], preferred_element_type=F32)
        first = block_take if block % 2 == 0 else pltpu.roll(block_take, TOK_MB, 1)
        take_ref[block] = first.astype(BF16)
        stacked = jnp.concatenate([first, first, eye], axis=0)
        place_ref[block] = jnp.transpose(stacked)[:TOK_MB, :].astype(BF16)
        picked = jnp.where(slot_bucket.astype(jnp.int32) == entry_no, 1.0, 0.0).astype(BF16)
        scale_rows = 1.0 + jnp.dot(picked, tables[0], preferred_element_type=F32)
        gate_rows = jnp.dot(picked, tables[1], preferred_element_type=F32)
        gate_ref[block] = slot_gate * gate_rows
        centred = raw - jnp.mean(raw, axis=-1, keepdims=True)
        inv_std = lax.rsqrt(jnp.mean(centred * centred, axis=-1, keepdims=True) + EPSILON)
        normed = centred * inv_std
        normed_ref[block] = normed
        scale_ref[block] = scale_rows * inv_std
        inputs = (normed * scale_rows).astype(BF16)
        for expert in range(experts):
            rows_ref[expert, block * CAP : (block + 1) * CAP, :] = inputs[
                expert * CAP : (expert + 1) * CAP, :
            ]
    copies[6].wait()
    for expert in range(experts):
        pre_act = jnp.dot(rows_ref[expert], up_ref[expert], preferred_element_type=F32)
        root = 0.7978845608028654
        square = pre_act * pre_act
        bend = jnp.tanh(root * (pre_act + 0.044715 * (square * pre_act)))
        half = 0.5 * (1.0 + bend)
        hidden_ref[expert] = (pre_act * half).astype(BF16)
        slope = half + 0.5 * pre_act * (1.0 - bend * bend) * (root * (1.0 + 0.134145 * square))
        slope_ref[expert] = slope.reshape(slope_ref.shape[1:])
    for copy in copies[7:]:
        copy.wait()


def prepare(act, ids, prob, bucket, scale_table, gate_table, up_mats, down_mats, out_grad):
    tokens, features = act.shape
    experts, _, width = up_mats.shape
    blocks = tokens // TOK_MB
    slots = experts * CAP
    top = out_grad.reshape(blocks, TOK_MB, features)
    values = (act, ids, prob, bucket, scale_table, gate_table, up_mats, down_mats, top)
    out_shape = (
        kept_shape(top.shape, BF16),
        kept_shape((blocks, slots, 2 * TOK_MB), BF16),
        kept_shape((blocks, TOK_MB, 2 * slots + TOK_MB), BF16),
        kept_shape((blocks, slots, features), F32),
        kept_shape((blocks, slots, features), F32),
        kept_shape((blocks, slots, features), F32),
        kept_shape((experts, blocks, CAP, width), F32),
        kept_shape(down_mats.shape, BF16),
        kept_shape(up_mats.shape, BF16),
        kept_shape((blocks, TOK_MB, features), BF16),
        kept_shape((experts, blocks, CAP, features), BF16),
        kept_shape((experts, blocks, CAP, width), BF16),
        kept_shape((TOK_MB, features), BF16),
        kept_shape((experts, blocks * CAP, width), BF16),
        kept_shape((experts, blocks * CAP, features), BF16),
    )
    return pl.pallas_call(
        prepare_kernel,
        out_shape=out_shape,
        in_specs=[pl.BlockSpec(memory_space=pltpu.HBM)] * len(values),
        out_specs=tuple(vmem_specs(len(out_shape))),
        scratch_shapes=[pltpu.VMEM(v.shape, v.dtype) for v in values[:6]]
        + [pltpu.SemaphoreType.DMA((len(values),))],
        compiler_params=pltpu.CompilerParams(vmem_limit_bytes=VMEM_LIMIT),
    )(*[pltpu.with_memory_space_constraint(v, pltpu.HBM) for v in values])


def step_kernel(
    cycle,
    parity,
    dot,
    given_ref,
    top_ref,
    take_ref,
    place_ref,
    gate_ref,
    scale_ref,
    normed_ref,
    slope_ref,
    down_ref,
    up_ref,
    _grad_in,
    _outs_in,
    _pres_in,
    grad_ref,
    outs_ref,
    pres_ref,
    *sent_refs,
):
    experts = down_ref.shape[0]
    blocks = take_ref.shape[0]
    depth = lax.axis_size("pipe") - 1 - lax.axis_index("pipe")
    block = block_of(cycle, depth)

    @pl.when((depth % 2 == parity) & (block >= 0) & (block < blocks))
    def _():
        grad_out = jnp.where(depth == 0, top_ref[block], given_ref[...])
        gathered = jnp.dot(take_ref[block][:, :TOK_MB], grad_out, preferred_element_type=F32)
        outs = (gate_ref[block] * gathered).astype(BF16)
        back = []
        for expert in range(experts):
            rows = slice(expert * CAP, (expert + 1) * CAP)
            outs_ref[expert, block] = outs[rows, :]
            hid_grad = dot(outs[rows, :], down_ref[expert])
            pres = (hid_grad * slope_ref[expert, block]).astype(BF16)
            pres_ref[expert, block] = pres
            back.append(dot(pres, up_ref[expert]))
        varied = jnp.concatenate(back, axis=0) * scale_ref[block]
        normed = normed_ref[block]
        lifted = (
            varied
            - jnp.mean(varied, axis=-1, keepdims=True)
            - normed * jnp.mean(varied * normed, axis=-1, keepdims=True)
        )
        high = lifted.astype(BF16)
        low = (lifted - high.astype(F32)).astype(BF16)
        parts = jnp.concatenate([high, low, grad_out], axis=0)
        grad_in = jnp.dot(place_ref[block], parts, preferred_element_type=F32).astype(BF16)
        for sent_ref in sent_refs:
            sent_ref[...] = grad_in
        grad_ref[block] = grad_in


def turned_dot(left, right):
    return lax.dot_general(left, right, (((1,), (1,)), ((), ())), preferred_element_type=F32)


def plain_dot(left, right):
    return jnp.dot(left, right, preferred_element_type=F32)


def turn_kernel(down_ref, up_ref, _pres_in, pres_ref, down_turned, up_turned):
    for source, target in ((down_ref, down_turned), (up_ref, up_turned)):
        for expert in range(source.shape[0]):
            target[expert] = jnp.transpose(source[expert])


def turn_mats(down_mats, up_mats, held):
    experts, width, features = down_mats.shape
    return pl.pallas_call(
        turn_kernel,
        out_shape=(
            kept_shape(held.shape, held.dtype),
            kept_shape((experts, features, width), BF16),
            kept_shape((experts, width, features), BF16),
        ),
        in_specs=vmem_specs(3),
        out_specs=tuple(vmem_specs(3)),
        input_output_aliases={2: 0},
        compiler_params=pltpu.CompilerParams(vmem_limit_bytes=VMEM_LIMIT),
    )(in_vmem(down_mats), in_vmem(up_mats), in_vmem(held))


def run_step(cycle, parity, dot, given, fixed, stores, sends):
    out_shape = stores + (given,) * sends
    count = 1 + len(fixed)
    return pl.pallas_call(
        functools.partial(step_kernel, cycle, parity, dot),
        out_shape=tuple(kept_shape(v.shape, v.dtype) for v in out_shape),
        in_specs=vmem_specs(count + len(stores)),
        out_specs=tuple(vmem_specs(len(out_shape))),
        input_output_aliases={count + i: i for i in range(len(stores))},
        compiler_params=pltpu.CompilerParams(vmem_limit_bytes=STEP_LIMIT),
    )(in_vmem(given), *[in_vmem(v) for v in fixed], *[in_vmem(v) for v in stores])


def block_of(cycle, depth):
    return cycle - depth // 2 * 3 - depth % 2


def run_chain(prepared):
    fixed, stores, given = prepared[:9], prepared[9:12], prepared[12]
    blocks = fixed[0].shape[0]
    sections = lax.axis_size("pipe")
    waiting = {0: [given, given], 1: [given]}
    cycles = sections // 2 * 3 + blocks
    for cycle in range(cycles):
        for parity in (0, 1):
            senders = [
                depth
                for depth in range(parity, sections, 2)
                if 0 <= block_of(cycle, depth) < blocks
            ]
            came = waiting[parity].pop(0)
            if not senders:
                waiting[1 - parity].append(came)
                continue
            window = 8
            first = senders[0] // window * window
            last = (senders[-1] // window + 1) * window
            depths = range(first + parity, min(last, sections - 1), 2)
            pairs = [(sections - 1 - d, sections - 2 - d) for d in depths]
            if senders[0] >= sections - 1:
                pairs = []
            dot = turned_dot if cycle == 0 else plain_dot
            results = run_step(cycle, parity, dot, came, fixed, stores, len(pairs) > 0)
            stores = results[:3]
            if cycle == 0:
                held, *mats = turn_mats(*fixed[-2:], stores[2])
                fixed, stores = fixed[:-2] + tuple(mats), stores[:2] + (held,)
            if pairs:
                came = lax.ppermute(results[3], "pipe", pairs)
            waiting[1 - parity].append(came)
    return tuple(stores)


def grads_kernel(rows_ref, pres_ref, hidden_ref, outs_ref, keep_ref, send_ref):
    experts, blocks, cap, features = outs_ref.shape
    chunk = keep_ref.shape[2]
    tile = max(256, 2 * chunk)
    core = lax.axis_index("dp") % 2
    terms = []
    for e in range(experts):
        terms.append((rows_ref[e], pres_ref[e].reshape(blocks * cap, -1)))
    for e in range(experts):
        terms.append((outs_ref[e].reshape(blocks * cap, features), hidden_ref[e]))
    for number, (left, right) in enumerate(terms):
        for start in range(0, features, tile):
            part = lax.dot_general(
                left[:, start : start + tile],
                right,
                (((0,), (0,)), ((), ())),
                preferred_element_type=F32,
            ).astype(BF16)
            for pair in range(tile // (2 * chunk)):
                place = start // (2 * chunk) + pair
                low = part[2 * pair * chunk : (2 * pair + 1) * chunk]
                high = part[(2 * pair + 1) * chunk : (2 * pair + 2) * chunk]
                keep_ref[place, number] = jnp.where(core == 0, low, high)
                send_ref[place, number] = jnp.where(core == 0, high, low)


def expert_grads(rows, pres, hidden, outs, owners):
    experts, _, features = rows.shape
    width = pres.shape[-1]
    shape = (owners // 2, 2 * experts, features // owners, width)
    return pl.pallas_call(
        grads_kernel,
        out_shape=(kept_shape(shape, BF16),) * 2,
        in_specs=vmem_specs(4),
        out_specs=tuple(vmem_specs(2)),
        compiler_params=pltpu.CompilerParams(vmem_limit_bytes=VMEM_LIMIT),
    )(in_vmem(rows), in_vmem(pres), in_vmem(hidden), in_vmem(outs))


def split_x_kernel(along_x, keep_ref, came_ref, own_ref, right_ref, left_ref, next_ref, past_ref):
    my_x = lax.axis_index("dp") // 2 % along_x
    half = right_ref.shape[2]
    for row in range(own_ref.shape[0]):
        parts = []
        for ahead in range(along_x):
            place = row * along_x + (my_x + ahead) % along_x
            part = keep_ref[place].astype(F32) + came_ref[place].astype(F32)
            parts.append(part.astype(BF16))
        own_ref[row] = parts[0]
        right_ref[0, row] = parts[2][:half]
        right_ref[1, row] = parts[1][half:]
        left_ref[0, row] = parts[2][half:]
        left_ref[1, row] = parts[3][:half]
        next_ref[row] = parts[1][:half]
        past_ref[row] = parts[3][half:]


def relay_kernel(next_ref, past_ref, from_left_ref, from_right_ref, right_ref, left_ref):
    right_ref[...] = (next_ref[...].astype(F32) + from_left_ref[0].astype(F32)).astype(BF16)
    left_ref[...] = (past_ref[...].astype(F32) + from_right_ref[0].astype(F32)).astype(BF16)


def split_y_kernel(own_ref, first_left, first_right, left_ref, right_ref, *part_refs):
    along_y = len(part_refs)
    half = left_ref.shape[1]
    my_y = lax.axis_index("dp") // (lax.axis_size("dp") // along_y)
    for ahead, part_ref in enumerate(part_refs):
        row = (my_y + ahead) % along_y
        low = left_ref[row].astype(F32) + first_right[1, row].astype(F32)
        high = right_ref[row].astype(F32) + first_left[1, row].astype(F32)
        total = own_ref[row].astype(F32)
        part_ref[:half] = (total[:half] + low).astype(part_ref.dtype)
        part_ref[half:] = (total[half:] + high).astype(part_ref.dtype)


def finish_kernel(own_ref, *refs):
    came_refs, (up_ref, down_ref) = refs[:-2], refs[-2:]
    experts = up_ref.shape[0]
    for number in range(2 * experts):
        total = own_ref[number]
        for came_ref in came_refs:
            total = total + came_ref[number].astype(F32)
        if number < experts:
            up_ref[number] = total
        else:
            down_ref[number - experts] = jnp.transpose(total)


def call_in_vmem(kernel, out_shape, *values):
    return pl.pallas_call(
        kernel,
        out_shape=out_shape,
        in_specs=vmem_specs(len(values)),
        out_specs=tuple(vmem_specs(len(out_shape))),
        compiler_params=pltpu.CompilerParams(vmem_limit_bytes=VMEM_LIMIT),
    )(*[in_vmem(v) for v in values])


def reduce_to_owner(keep, send):
    owners = lax.axis_size("dp")
    along_x = 4
    along_y = owners // (2 * along_x)
    _, terms, chunk, width = keep.shape

    def move_x(ahead):
        return [
            (d, d - 2 * (d // 2 % along_x) + 2 * ((d // 2 + ahead) % along_x)) for d in range(owners)
        ]

    def move_y(ahead):
        return [(d, (d + ahead * 2 * along_x) % owners) for d in range(owners)]

    came = lax.ppermute(send, "dp", [(d, d ^ 1) for d in range(owners)])
    half = terms // 2
    whole = kept_shape((along_y, terms, chunk, width), BF16)
    double = kept_shape((2, along_y, half, chunk, width), BF16)
    single = kept_shape((along_y, half, chunk, width), BF16)
    own, right, left, following, past = call_in_vmem(
        functools.partial(split_x_kernel, along_x),
        (whole, double, double, single, single),
        keep,
        came,
    )
    first_left = lax.ppermute(right, "dp", move_x(1))
    first_right = lax.ppermute(left, "dp", move_x(-1))
    right, left = call_in_vmem(
        relay_kernel, (single, single), following, past, first_left, first_right
    )
    last_left = lax.ppermute(right, "dp", move_x(1))
    last_right = lax.ppermute(left, "dp", move_x(-1))
    shape = (terms, chunk, width)
    shapes = (kept_shape(shape, F32),) + (kept_shape(shape, BF16),) * (along_y - 1)
    own, *others = call_in_vmem(
        split_y_kernel, shapes, own, first_left, first_right, last_left, last_right
    )
    others = [lax.ppermute(v, "dp", move_y(i + 1)) for i, v in enumerate(others)]
    shapes = (
        jax.ShapeDtypeStruct((terms // 2, chunk, width), F32),
        jax.ShapeDtypeStruct((terms // 2, width, chunk), F32),
    )
    return call_in_vmem(finish_kernel, shapes, own, *others)


def per_device(
    activations, out_grad, w_up, w_down, mod_scale, mod_gate, expert_ids, gate_prob, bucket
):
    features = activations.shape[2]
    prepared = prepare(
        activations[0],
        expert_ids[0].T,
        gate_prob[0].T,
        bucket[None, :],
        mod_scale[0],
        mod_gate[0],
        w_up[0],
        w_down[0],
        out_grad,
    )
    grads, outs, pres = run_chain(prepared)
    hidden, rows = prepared[13:]
    keep, send = expert_grads(rows, pres, hidden, outs, lax.axis_size("dp"))
    up_shard, down_shard = reduce_to_owner(keep, send)
    return (grads.reshape(1, -1, features), up_shard[None], down_shard[None])


def solution(mesh):
    return jax.shard_map(
        per_device,
        mesh=mesh,
        in_specs=(
            P("pipe", "dp", None),
            P("dp", None),
            P("pipe", None, None, None),
            P("pipe", None, None, None),
            P("pipe", None, None),
            P("pipe", None, None),
            P("pipe", "dp", None),
            P("pipe", "dp", None),
            P("dp"),
        ),
        out_specs=(P("pipe", "dp", None), P("pipe", None, "dp", None), P("pipe", None, None, "dp")),
        check_vma=False,
    )
```

```python
import functools

import jax
import jax.numpy as jnp
from jax import lax
from jax.experimental import pallas as pl
from jax.experimental.pallas import tpu as pltpu
from jax.sharding import PartitionSpec as P

TOK_MB = 64
CAP = 16
EPSILON = 1e-06
F32 = jnp.float32
BF16 = jnp.bfloat16
VMEM_LIMIT = 24 * 1024 * 1024
LAG_EVEN = 2
LAG_ODD = 1
STEP_LIMIT = 6 * 1024 * 1024


def in_vmem(value):
    return pltpu.with_memory_space_constraint(value, pltpu.VMEM)


def kept_shape(shape, dtype):
    return pltpu.VMEM(shape, dtype)


def vmem_specs(count):
    return [pl.BlockSpec(memory_space=pltpu.VMEM)] * count


def three_parts(table):
    high = table.astype(BF16)
    rest = table - high.astype(F32)
    middle = rest.astype(BF16)
    low = (rest - middle.astype(F32)).astype(BF16)
    return jnp.concatenate([high, middle, low], axis=0)


def prepare_kernel(
    act_hbm,
    ids_hbm,
    prob_hbm,
    bucket_hbm,
    scale_hbm,
    gate_hbm,
    up_hbm,
    down_hbm,
    top_hbm,
    top_ref,
    take_ref,
    place_ref,
    gate_ref,
    scale_ref,
    normed_ref,
    slope_ref,
    down_ref,
    up_ref,
    _grad_store,
    _outs_store,
    _pres_store,
    _given,
    hidden_ref,
    rows_ref,
    act_ref,
    ids_ref,
    prob_ref,
    bucket_ref,
    scale_table_ref,
    gate_table_ref,
    sems,
):
    moves = [
        (ids_hbm, ids_ref),
        (prob_hbm, prob_ref),
        (bucket_hbm, bucket_ref),
        (scale_hbm, scale_table_ref),
        (gate_hbm, gate_table_ref),
        (act_hbm, act_ref),
        (up_hbm, up_ref),
        (top_hbm, top_ref),
        (down_hbm, down_ref),
    ]
    copies = [
        pltpu.make_async_copy(source, target, sems.at[number])
        for number, (source, target) in enumerate(moves)
    ]
    for copy in copies:
        copy.start()
    for copy in copies[:3]:
        copy.wait()
    tokens = act_ref.shape[0]
    experts = up_ref.shape[0]
    slots = experts * CAP
    features = act_ref.shape[1]
    ids = ids_ref[...]
    prob = prob_ref[...]
    bucket = bucket_ref[...].astype(F32)
    lane = lax.broadcasted_iota(jnp.int32, (1, tokens), 1) % TOK_MB
    slot_no = (lax.broadcasted_iota(jnp.int32, (CAP, tokens), 0) + 1).astype(F32)
    hits = []
    gates = []
    for expert in range(experts):
        chosen = ids == expert
        routed = jnp.max(jnp.where(chosen, 1.0, 0.0), axis=0, keepdims=True)
        token_gate = jnp.sum(jnp.where(chosen, prob, 0.0), axis=0, keepdims=True)
        place = routed
        step = 1
        while step < TOK_MB:
            place = place + jnp.where(lane >= step, pltpu.roll(place, step, 1), 0.0)
            step *= 2
        hit = jnp.where((place == slot_no) & (routed > 0.0), 1.0, 0.0)
        hits.append(hit)
        gates.append(hit * token_gate)
    take = jnp.concatenate(hits, axis=0)
    gates = jnp.concatenate(gates, axis=0)
    buckets = take * bucket
    for copy in copies[3:6]:
        copy.wait()
    tables = three_parts(scale_table_ref[...]), three_parts(gate_table_ref[...])
    entries = scale_table_ref.shape[0]
    wide = lax.broadcasted_iota(jnp.int32, (slots, 2 * TOK_MB), 1)
    eye = jnp.where(
        lax.broadcasted_iota(jnp.int32, (TOK_MB, 2 * TOK_MB), 0)
        == lax.broadcasted_iota(jnp.int32, (TOK_MB, 2 * TOK_MB), 1),
        1.0,
        0.0,
    )
    entry_no = lax.broadcasted_iota(jnp.int32, (slots, 3 * entries), 1) % entries
    for block in range(tokens // TOK_MB):
        pair = slice(block // 2 * 2 * TOK_MB, (block // 2 + 1) * 2 * TOK_MB)
        inside = (wide < TOK_MB) if block % 2 == 0 else (wide >= TOK_MB)
        block_take = jnp.where(inside, take[:, pair], 0.0)
        slot_gate = jnp.sum(jnp.where(inside, gates[:, pair], 0.0), axis=1, keepdims=True)
        slot_bucket = jnp.sum(jnp.where(inside, buckets[:, pair], 0.0), axis=1, keepdims=True)
        raw = jnp.dot(block_take.astype(BF16), act_ref[pair, :], preferred_element_type=F32)
        first = block_take if block % 2 == 0 else pltpu.roll(block_take, TOK_MB, 1)
        take_ref[block] = first.astype(BF16)
        stacked = jnp.concatenate([first, first, eye], axis=0)
        place_ref[block] = jnp.transpose(stacked)[:TOK_MB, :].astype(BF16)
        picked = jnp.where(slot_bucket.astype(jnp.int32) == entry_no, 1.0, 0.0).astype(BF16)
        scale_rows = 1.0 + jnp.dot(picked, tables[0], preferred_element_type=F32)
        gate_rows = jnp.dot(picked, tables[1], preferred_element_type=F32)
        gate_ref[block] = slot_gate * gate_rows
        centred = raw - jnp.mean(raw, axis=-1, keepdims=True)
        inv_std = lax.rsqrt(jnp.mean(centred * centred, axis=-1, keepdims=True) + EPSILON)
        normed = centred * inv_std
        normed_ref[block] = normed
        scale_ref[block] = scale_rows * inv_std
        inputs = (normed * scale_rows).astype(BF16)
        for expert in range(experts):
            rows_ref[expert, block * CAP : (block + 1) * CAP, :] = inputs[
                expert * CAP : (expert + 1) * CAP, :
            ]
    copies[6].wait()
    for expert in range(experts):
        pre_act = jnp.dot(rows_ref[expert], up_ref[expert], preferred_element_type=F32)
        root = 0.7978845608028654
        square = pre_act * pre_act
        bend = jnp.tanh(root * (pre_act + 0.044715 * (square * pre_act)))
        half = 0.5 * (1.0 + bend)
        hidden_ref[expert] = (pre_act * half).astype(BF16)
        slope = half + 0.5 * pre_act * (1.0 - bend * bend) * (root * (1.0 + 0.134145 * square))
        slope_ref[expert] = slope.reshape(slope_ref.shape[1:])
    for copy in copies[7:]:
        copy.wait()


def prepare(act, ids, prob, bucket, scale_table, gate_table, up_mats, down_mats, out_grad):
    tokens, features = act.shape
    experts, _, width = up_mats.shape
    blocks = tokens // TOK_MB
    slots = experts * CAP
    top = out_grad.reshape(blocks, TOK_MB, features)
    values = (act, ids, prob, bucket, scale_table, gate_table, up_mats, down_mats, top)
    out_shape = (
        kept_shape(top.shape, BF16),
        kept_shape((blocks, slots, 2 * TOK_MB), BF16),
        kept_shape((blocks, TOK_MB, 2 * slots + TOK_MB), BF16),
        kept_shape((blocks, slots, features), F32),
        kept_shape((blocks, slots, features), F32),
        kept_shape((blocks, slots, features), F32),
        kept_shape((experts, blocks, CAP, width), F32),
        kept_shape(down_mats.shape, BF16),
        kept_shape(up_mats.shape, BF16),
        kept_shape((blocks, TOK_MB, features), BF16),
        kept_shape((experts, blocks, CAP, features), BF16),
        kept_shape((experts, blocks, CAP, width), BF16),
        kept_shape((TOK_MB, features), BF16),
        kept_shape((experts, blocks * CAP, width), BF16),
        kept_shape((experts, blocks * CAP, features), BF16),
    )
    return pl.pallas_call(
        prepare_kernel,
        out_shape=out_shape,
        in_specs=[pl.BlockSpec(memory_space=pltpu.HBM)] * len(values),
        out_specs=tuple(vmem_specs(len(out_shape))),
        scratch_shapes=[pltpu.VMEM(v.shape, v.dtype) for v in values[:6]]
        + [pltpu.SemaphoreType.DMA((len(values),))],
        compiler_params=pltpu.CompilerParams(vmem_limit_bytes=VMEM_LIMIT),
    )(*[pltpu.with_memory_space_constraint(v, pltpu.HBM) for v in values])


def step_kernel(
    cycle,
    parity,
    dot,
    given_ref,
    top_ref,
    take_ref,
    place_ref,
    gate_ref,
    scale_ref,
    normed_ref,
    slope_ref,
    down_ref,
    up_ref,
    _grad_in,
    _outs_in,
    _pres_in,
    grad_ref,
    outs_ref,
    pres_ref,
    *sent_refs,
):
    experts = down_ref.shape[0]
    blocks = take_ref.shape[0]
    depth = lax.axis_size("pipe") - 1 - lax.axis_index("pipe")
    block = block_of(cycle, depth)

    @pl.when((depth % 2 == parity) & (block >= 0) & (block < blocks))
    def _():
        grad_out = jnp.where(depth == 0, top_ref[block], given_ref[...])
        gathered = jnp.dot(take_ref[block][:, :TOK_MB], grad_out, preferred_element_type=F32)
        outs = (gate_ref[block] * gathered).astype(BF16)
        back = []
        for expert in range(experts):
            rows = slice(expert * CAP, (expert + 1) * CAP)
            outs_ref[expert, block] = outs[rows, :]
            hid_grad = dot(outs[rows, :], down_ref[expert])
            pres = (hid_grad * slope_ref[expert, block]).astype(BF16)
            pres_ref[expert, block] = pres
            back.append(dot(pres, up_ref[expert]))
        varied = jnp.concatenate(back, axis=0) * scale_ref[block]
        normed = normed_ref[block]
        lifted = (
            varied
            - jnp.mean(varied, axis=-1, keepdims=True)
            - normed * jnp.mean(varied * normed, axis=-1, keepdims=True)
        )
        high = lifted.astype(BF16)
        low = (lifted - high.astype(F32)).astype(BF16)
        parts = jnp.concatenate([high, low, grad_out], axis=0)
        grad_in = jnp.dot(place_ref[block], parts, preferred_element_type=F32).astype(BF16)
        for sent_ref in sent_refs:
            sent_ref[...] = grad_in
        grad_ref[block] = grad_in


def turned_dot(left, right):
    return lax.dot_general(left, right, (((1,), (1,)), ((), ())), preferred_element_type=F32)


def plain_dot(left, right):
    return jnp.dot(left, right, preferred_element_type=F32)


def turn_kernel(down_ref, up_ref, _pres_in, pres_ref, down_turned, up_turned):
    for source, target in ((down_ref, down_turned), (up_ref, up_turned)):
        for expert in range(source.shape[0]):
            target[expert] = jnp.transpose(source[expert])


def turn_mats(down_mats, up_mats, held):
    experts, width, features = down_mats.shape
    return pl.pallas_call(
        turn_kernel,
        out_shape=(
            kept_shape(held.shape, held.dtype),
            kept_shape((experts, features, width), BF16),
            kept_shape((experts, width, features), BF16),
        ),
        in_specs=vmem_specs(3),
        out_specs=tuple(vmem_specs(3)),
        input_output_aliases={2: 0},
        compiler_params=pltpu.CompilerParams(vmem_limit_bytes=VMEM_LIMIT),
    )(in_vmem(down_mats), in_vmem(up_mats), in_vmem(held))


def run_step(cycle, parity, dot, given, fixed, stores, sends):
    out_shape = stores + (given,) * sends
    count = 1 + len(fixed)
    return pl.pallas_call(
        functools.partial(step_kernel, cycle, parity, dot),
        out_shape=tuple(kept_shape(v.shape, v.dtype) for v in out_shape),
        in_specs=vmem_specs(count + len(stores)),
        out_specs=tuple(vmem_specs(len(out_shape))),
        input_output_aliases={count + i: i for i in range(len(stores))},
        compiler_params=pltpu.CompilerParams(vmem_limit_bytes=STEP_LIMIT),
    )(in_vmem(given), *[in_vmem(v) for v in fixed], *[in_vmem(v) for v in stores])


def block_of(cycle, depth):
    return cycle - depth // 2 * (LAG_EVEN + LAG_ODD) - depth % 2 * LAG_ODD


def span_of(last):
    if last < 12:
        return 0, (last // 4 + 1) * 4
    return (6, 18) if last < 18 else (12, 24)


def run_chain(prepared):
    fixed, stores, given = prepared[:9], prepared[9:12], prepared[12]
    blocks = fixed[0].shape[0]
    sections = lax.axis_size("pipe")
    waiting = {0: [given] * LAG_EVEN, 1: [given] * LAG_ODD}
    cycles = sections // 2 * (LAG_EVEN + LAG_ODD) + blocks
    for cycle in range(cycles):
        for parity in (0, 1):
            senders = [
                depth
                for depth in range(parity, sections, 2)
                if 0 <= block_of(cycle, depth) < blocks
            ]
            came = waiting[parity].pop(0)
            if not senders:
                waiting[1 - parity].append(came)
                continue
            first, last = span_of(senders[-1])
            depths = range(first + parity, min(last, sections - 1), 2)
            pairs = [(sections - 1 - d, sections - 2 - d) for d in depths]
            if senders[0] >= sections - 1:
                pairs = []
            dot = turned_dot if cycle == 0 else plain_dot
            results = run_step(cycle, parity, dot, came, fixed, stores, len(pairs) > 0)
            stores = results[:3]
            if cycle == 0:
                held, *mats = turn_mats(*fixed[-2:], stores[2])
                fixed, stores = fixed[:-2] + tuple(mats), stores[:2] + (held,)
            if pairs:
                came = lax.ppermute(results[3], "pipe", pairs)
            waiting[1 - parity].append(came)
    return tuple(stores)


def grads_kernel(rows_ref, pres_ref, hidden_ref, outs_ref, keep_ref, send_ref):
    experts, blocks, cap, features = outs_ref.shape
    chunk = keep_ref.shape[2]
    tile = max(256, 2 * chunk)
    core = lax.axis_index("dp") % 2
    terms = []
    for e in range(experts):
        terms.append((rows_ref[e], pres_ref[e].reshape(blocks * cap, -1)))
    for e in range(experts):
        terms.append((outs_ref[e].reshape(blocks * cap, features), hidden_ref[e]))
    for number, (left, right) in enumerate(terms):
        for start in range(0, features, tile):
            part = lax.dot_general(
                left[:, start : start + tile],
                right,
                (((0,), (0,)), ((), ())),
                preferred_element_type=F32,
            ).astype(BF16)
            for pair in range(tile // (2 * chunk)):
                place = start // (2 * chunk) + pair
                low = part[2 * pair * chunk : (2 * pair + 1) * chunk]
                high = part[(2 * pair + 1) * chunk : (2 * pair + 2) * chunk]
                keep_ref[place, number] = jnp.where(core == 0, low, high)
                send_ref[place, number] = jnp.where(core == 0, high, low)


def expert_grads(rows, pres, hidden, outs, owners):
    experts, _, features = rows.shape
    width = pres.shape[-1]
    shape = (owners // 2, 2 * experts, features // owners, width)
    return pl.pallas_call(
        grads_kernel,
        out_shape=(kept_shape(shape, BF16),) * 2,
        in_specs=vmem_specs(4),
        out_specs=tuple(vmem_specs(2)),
        compiler_params=pltpu.CompilerParams(vmem_limit_bytes=VMEM_LIMIT),
    )(in_vmem(rows), in_vmem(pres), in_vmem(hidden), in_vmem(outs))


def split_x_kernel(along_x, keep_ref, came_ref, own_ref, right_ref, left_ref, next_ref, past_ref):
    my_x = lax.axis_index("dp") // 2 % along_x
    half = right_ref.shape[2]
    for row in range(own_ref.shape[0]):
        parts = []
        for ahead in range(along_x):
            place = row * along_x + (my_x + ahead) % along_x
            part = keep_ref[place].astype(F32) + came_ref[place].astype(F32)
            parts.append(part.astype(BF16))
        own_ref[row] = parts[0]
        right_ref[0, row] = parts[2][:half]
        right_ref[1, row] = parts[1][half:]
        left_ref[0, row] = parts[2][half:]
        left_ref[1, row] = parts[3][:half]
        next_ref[row] = parts[1][:half]
        past_ref[row] = parts[3][half:]


def relay_kernel(next_ref, past_ref, from_left_ref, from_right_ref, right_ref, left_ref):
    right_ref[...] = (next_ref[...].astype(F32) + from_left_ref[0].astype(F32)).astype(BF16)
    left_ref[...] = (past_ref[...].astype(F32) + from_right_ref[0].astype(F32)).astype(BF16)


def split_y_kernel(own_ref, first_left, first_right, left_ref, right_ref, *part_refs):
    along_y = len(part_refs)
    half = left_ref.shape[1]
    my_y = lax.axis_index("dp") // (lax.axis_size("dp") // along_y)
    for ahead, part_ref in enumerate(part_refs):
        row = (my_y + ahead) % along_y
        low = left_ref[row].astype(F32) + first_right[1, row].astype(F32)
        high = right_ref[row].astype(F32) + first_left[1, row].astype(F32)
        total = own_ref[row].astype(F32)
        part_ref[:half] = (total[:half] + low).astype(part_ref.dtype)
        part_ref[half:] = (total[half:] + high).astype(part_ref.dtype)


def finish_kernel(own_ref, *refs):
    came_refs, (up_ref, down_ref) = refs[:-2], refs[-2:]
    experts = up_ref.shape[0]
    for number in range(2 * experts):
        total = own_ref[number]
        for came_ref in came_refs:
            total = total + came_ref[number].astype(F32)
        if number < experts:
            up_ref[number] = total
        else:
            down_ref[number - experts] = total


def call_in_vmem(kernel, out_shape, *values):
    return pl.pallas_call(
        kernel,
        out_shape=out_shape,
        in_specs=vmem_specs(len(values)),
        out_specs=tuple(vmem_specs(len(out_shape))),
        compiler_params=pltpu.CompilerParams(vmem_limit_bytes=VMEM_LIMIT),
    )(*[in_vmem(v) for v in values])


def reduce_to_owner(keep, send):
    owners = lax.axis_size("dp")
    along_x = 4
    along_y = owners // (2 * along_x)
    _, terms, chunk, width = keep.shape

    def move_x(ahead):
        return [
            (d, d - 2 * (d // 2 % along_x) + 2 * ((d // 2 + ahead) % along_x)) for d in range(owners)
        ]

    def move_y(ahead):
        return [(d, (d + ahead * 2 * along_x) % owners) for d in range(owners)]

    came = lax.ppermute(send, "dp", [(d, d ^ 1) for d in range(owners)])
    half = terms // 2
    whole = kept_shape((along_y, terms, chunk, width), BF16)
    double = kept_shape((2, along_y, half, chunk, width), BF16)
    single = kept_shape((along_y, half, chunk, width), BF16)
    own, right, left, following, past = call_in_vmem(
        functools.partial(split_x_kernel, along_x),
        (whole, double, double, single, single),
        keep,
        came,
    )
    first_left = lax.ppermute(right, "dp", move_x(1))
    first_right = lax.ppermute(left, "dp", move_x(-1))
    right, left = call_in_vmem(
        relay_kernel, (single, single), following, past, first_left, first_right
    )
    last_left = lax.ppermute(right, "dp", move_x(1))
    last_right = lax.ppermute(left, "dp", move_x(-1))
    shape = (terms, chunk, width)
    shapes = (kept_shape(shape, F32),) + (kept_shape(shape, BF16),) * (along_y - 1)
    own, *others = call_in_vmem(
        split_y_kernel, shapes, own, first_left, first_right, last_left, last_right
    )
    others = [lax.ppermute(v, "dp", move_y(i + 1)) for i, v in enumerate(others)]
    shapes = (jax.ShapeDtypeStruct((half, chunk, width), F32),) * 2
    up_shard, down_shard = call_in_vmem(finish_kernel, shapes, own, *others)
    return up_shard, jnp.swapaxes(down_shard, 1, 2)


def per_device(
    activations, out_grad, w_up, w_down, mod_scale, mod_gate, expert_ids, gate_prob, bucket
):
    features = activations.shape[2]
    prepared = prepare(
        activations[0],
        expert_ids[0].T,
        gate_prob[0].T,
        bucket[None, :],
        mod_scale[0],
        mod_gate[0],
        w_up[0],
        w_down[0],
        out_grad,
    )
    grads, outs, pres = run_chain(prepared)
    hidden, rows = prepared[13:]
    keep, send = expert_grads(rows, pres, hidden, outs, lax.axis_size("dp"))
    up_shard, down_shard = reduce_to_owner(keep, send)
    return (grads.reshape(1, -1, features), up_shard[None], down_shard[None])


def solution(mesh):
    return jax.shard_map(
        per_device,
        mesh=mesh,
        in_specs=(
            P("pipe", "dp", None),
            P("dp", None),
            P("pipe", None, None, None),
            P("pipe", None, None, None),
            P("pipe", None, None),
            P("pipe", None, None),
            P("pipe", "dp", None),
            P("pipe", "dp", None),
            P("dp"),
        ),
        out_specs=(P("pipe", "dp", None), P("pipe", None, "dp", None), P("pipe", None, None, "dp")),
        check_vma=False,
    )
```

```python
import functools

import jax
import jax.numpy as jnp
from jax import lax
from jax.experimental import pallas as pl
from jax.experimental.pallas import tpu as pltpu
from jax.sharding import PartitionSpec as P

TOK_MB = 64
CAP = 16
EPSILON = 1e-06
F32 = jnp.float32
BF16 = jnp.bfloat16
VMEM_LIMIT = 24 * 1024 * 1024
LAG_EVEN = 2
LAG_ODD = 1
STEP_LIMIT = 6 * 1024 * 1024


def in_vmem(value):
    return pltpu.with_memory_space_constraint(value, pltpu.VMEM)


def kept_shape(shape, dtype):
    return pltpu.VMEM(shape, dtype)


def vmem_specs(count):
    return [pl.BlockSpec(memory_space=pltpu.VMEM)] * count


def three_parts(table):
    high = table.astype(BF16)
    rest = table - high.astype(F32)
    middle = rest.astype(BF16)
    low = (rest - middle.astype(F32)).astype(BF16)
    return jnp.concatenate([high, middle, low], axis=0)


def prepare_kernel(
    act_hbm,
    ids_hbm,
    prob_hbm,
    bucket_hbm,
    scale_hbm,
    gate_hbm,
    up_hbm,
    down_hbm,
    top_hbm,
    top_ref,
    take_ref,
    place_ref,
    gate_ref,
    scale_ref,
    normed_ref,
    slope_ref,
    down_ref,
    up_ref,
    _grad_store,
    _outs_store,
    _pres_store,
    _given,
    hidden_ref,
    rows_ref,
    act_ref,
    ids_ref,
    prob_ref,
    bucket_ref,
    scale_table_ref,
    gate_table_ref,
    sems,
):
    moves = [
        (ids_hbm, ids_ref),
        (prob_hbm, prob_ref),
        (bucket_hbm, bucket_ref),
        (scale_hbm, scale_table_ref),
        (gate_hbm, gate_table_ref),
        (act_hbm, act_ref),
        (up_hbm, up_ref),
        (top_hbm, top_ref),
        (down_hbm, down_ref),
    ]
    copies = [
        pltpu.make_async_copy(source, target, sems.at[number])
        for number, (source, target) in enumerate(moves)
    ]
    for copy in copies:
        copy.start()
    for copy in copies[:3]:
        copy.wait()
    tokens = act_ref.shape[0]
    experts = up_ref.shape[0]
    slots = experts * CAP
    features = act_ref.shape[1]
    ids = ids_ref[...]
    prob = prob_ref[...]
    bucket = bucket_ref[...].astype(F32)
    lane = lax.broadcasted_iota(jnp.int32, (1, tokens), 1) % TOK_MB
    slot_no = (lax.broadcasted_iota(jnp.int32, (CAP, tokens), 0) + 1).astype(F32)
    hits = []
    gates = []
    for expert in range(experts):
        chosen = ids == expert
        routed = jnp.max(jnp.where(chosen, 1.0, 0.0), axis=0, keepdims=True)
        token_gate = jnp.sum(jnp.where(chosen, prob, 0.0), axis=0, keepdims=True)
        place = routed
        step = 1
        while step < TOK_MB:
            place = place + jnp.where(lane >= step, pltpu.roll(place, step, 1), 0.0)
            step *= 2
        hit = jnp.where((place == slot_no) & (routed > 0.0), 1.0, 0.0)
        hits.append(hit)
        gates.append(hit * token_gate)
    take = jnp.concatenate(hits, axis=0)
    gates = jnp.concatenate(gates, axis=0)
    buckets = take * bucket
    for copy in copies[3:6]:
        copy.wait()
    tables = three_parts(scale_table_ref[...]), three_parts(gate_table_ref[...])
    entries = scale_table_ref.shape[0]
    wide = lax.broadcasted_iota(jnp.int32, (slots, 2 * TOK_MB), 1)
    eye = jnp.where(
        lax.broadcasted_iota(jnp.int32, (TOK_MB, 2 * TOK_MB), 0)
        == lax.broadcasted_iota(jnp.int32, (TOK_MB, 2 * TOK_MB), 1),
        1.0,
        0.0,
    )
    entry_no = lax.broadcasted_iota(jnp.int32, (slots, 3 * entries), 1) % entries
    for block in range(tokens // TOK_MB):
        pair = slice(block // 2 * 2 * TOK_MB, (block // 2 + 1) * 2 * TOK_MB)
        inside = (wide < TOK_MB) if block % 2 == 0 else (wide >= TOK_MB)
        block_take = jnp.where(inside, take[:, pair], 0.0)
        slot_gate = jnp.sum(jnp.where(inside, gates[:, pair], 0.0), axis=1, keepdims=True)
        slot_bucket = jnp.sum(jnp.where(inside, buckets[:, pair], 0.0), axis=1, keepdims=True)
        raw = jnp.dot(block_take.astype(BF16), act_ref[pair, :], preferred_element_type=F32)
        first = block_take if block % 2 == 0 else pltpu.roll(block_take, TOK_MB, 1)
        take_ref[block] = first.astype(BF16)
        stacked = jnp.concatenate([first, first, eye], axis=0)
        place_ref[block] = jnp.transpose(stacked)[:TOK_MB, :].astype(BF16)
        picked = jnp.where(slot_bucket.astype(jnp.int32) == entry_no, 1.0, 0.0).astype(BF16)
        scale_rows = 1.0 + jnp.dot(picked, tables[0], preferred_element_type=F32)
        gate_rows = jnp.dot(picked, tables[1], preferred_element_type=F32)
        gate_ref[block] = slot_gate * gate_rows
        centred = raw - jnp.mean(raw, axis=-1, keepdims=True)
        inv_std = lax.rsqrt(jnp.mean(centred * centred, axis=-1, keepdims=True) + EPSILON)
        normed = centred * inv_std
        normed_ref[block] = normed
        scale_ref[block] = scale_rows * inv_std
        inputs = (normed * scale_rows).astype(BF16)
        for expert in range(experts):
            rows_ref[expert, block * CAP : (block + 1) * CAP, :] = inputs[
                expert * CAP : (expert + 1) * CAP, :
            ]
    copies[6].wait()
    for expert in range(experts):
        pre_act = jnp.dot(rows_ref[expert], up_ref[expert], preferred_element_type=F32)
        root = 0.7978845608028654
        square = pre_act * pre_act
        bend = jnp.tanh(root * (pre_act + 0.044715 * (square * pre_act)))
        half = 0.5 * (1.0 + bend)
        hidden_ref[expert] = (pre_act * half).astype(BF16)
        slope = half + 0.5 * pre_act * (1.0 - bend * bend) * (root * (1.0 + 0.134145 * square))
        slope_ref[expert] = slope.reshape(slope_ref.shape[1:])
    for copy in copies[7:]:
        copy.wait()


def prepare(act, ids, prob, bucket, scale_table, gate_table, up_mats, down_mats, out_grad):
    tokens, features = act.shape
    experts, _, width = up_mats.shape
    blocks = tokens // TOK_MB
    slots = experts * CAP
    top = out_grad.reshape(blocks, TOK_MB, features)
    values = (act, ids, prob, bucket, scale_table, gate_table, up_mats, down_mats, top)
    out_shape = (
        kept_shape(top.shape, BF16),
        kept_shape((blocks, slots, 2 * TOK_MB), BF16),
        kept_shape((blocks, TOK_MB, 2 * slots + TOK_MB), BF16),
        kept_shape((blocks, slots, features), F32),
        kept_shape((blocks, slots, features), F32),
        kept_shape((blocks, slots, features), F32),
        kept_shape((experts, blocks, CAP, width), F32),
        kept_shape(down_mats.shape, BF16),
        kept_shape(up_mats.shape, BF16),
        kept_shape((blocks, TOK_MB, features), BF16),
        kept_shape((experts, blocks, CAP, features), BF16),
        kept_shape((experts, blocks, CAP, width), BF16),
        kept_shape((TOK_MB, features), BF16),
        kept_shape((experts, blocks * CAP, width), BF16),
        kept_shape((experts, blocks * CAP, features), BF16),
    )
    return pl.pallas_call(
        prepare_kernel,
        out_shape=out_shape,
        in_specs=[pl.BlockSpec(memory_space=pltpu.HBM)] * len(values),
        out_specs=tuple(vmem_specs(len(out_shape))),
        scratch_shapes=[pltpu.VMEM(v.shape, v.dtype) for v in values[:6]]
        + [pltpu.SemaphoreType.DMA((len(values),))],
        compiler_params=pltpu.CompilerParams(vmem_limit_bytes=VMEM_LIMIT),
    )(*[pltpu.with_memory_space_constraint(v, pltpu.HBM) for v in values])


def step_kernel(
    cycle,
    parity,
    dot,
    given_ref,
    top_ref,
    take_ref,
    place_ref,
    gate_ref,
    scale_ref,
    normed_ref,
    slope_ref,
    down_ref,
    up_ref,
    _grad_in,
    _outs_in,
    _pres_in,
    grad_ref,
    outs_ref,
    pres_ref,
    *sent_refs,
):
    experts = down_ref.shape[0]
    blocks = take_ref.shape[0]
    depth = lax.axis_size("pipe") - 1 - lax.axis_index("pipe")
    block = block_of(cycle, depth)

    @pl.when((depth % 2 == parity) & (block >= 0) & (block < blocks))
    def _():
        grad_out = jnp.where(depth == 0, top_ref[block], given_ref[...])
        gathered = jnp.dot(take_ref[block][:, :TOK_MB], grad_out, preferred_element_type=F32)
        outs = (gate_ref[block] * gathered).astype(BF16)
        back = []
        for expert in range(experts):
            rows = slice(expert * CAP, (expert + 1) * CAP)
            outs_ref[expert, block] = outs[rows, :]
            hid_grad = dot(outs[rows, :], down_ref[expert])
            pres = (hid_grad * slope_ref[expert, block]).astype(BF16)
            pres_ref[expert, block] = pres
            back.append(dot(pres, up_ref[expert]))
        varied = jnp.concatenate(back, axis=0) * scale_ref[block]
        normed = normed_ref[block]
        lifted = (
            varied
            - jnp.mean(varied, axis=-1, keepdims=True)
            - normed * jnp.mean(varied * normed, axis=-1, keepdims=True)
        )
        high = lifted.astype(BF16)
        low = (lifted - high.astype(F32)).astype(BF16)
        parts = jnp.concatenate([high, low, grad_out], axis=0)
        grad_in = jnp.dot(place_ref[block], parts, preferred_element_type=F32).astype(BF16)
        for sent_ref in sent_refs:
            sent_ref[...] = grad_in
        grad_ref[block] = grad_in


def turned_dot(left, right):
    return lax.dot_general(left, right, (((1,), (1,)), ((), ())), preferred_element_type=F32)


def plain_dot(left, right):
    return jnp.dot(left, right, preferred_element_type=F32)


def turn_kernel(down_ref, up_ref, _pres_in, pres_ref, down_turned, up_turned):
    for source, target in ((down_ref, down_turned), (up_ref, up_turned)):
        for expert in range(source.shape[0]):
            target[expert] = jnp.transpose(source[expert])


def turn_mats(down_mats, up_mats, held):
    experts, width, features = down_mats.shape
    return pl.pallas_call(
        turn_kernel,
        out_shape=(
            kept_shape(held.shape, held.dtype),
            kept_shape((experts, features, width), BF16),
            kept_shape((experts, width, features), BF16),
        ),
        in_specs=vmem_specs(3),
        out_specs=tuple(vmem_specs(3)),
        input_output_aliases={2: 0},
        compiler_params=pltpu.CompilerParams(vmem_limit_bytes=VMEM_LIMIT),
    )(in_vmem(down_mats), in_vmem(up_mats), in_vmem(held))


def run_step(cycle, parity, dot, given, fixed, stores, sends):
    out_shape = stores + (given,) * sends
    count = 1 + len(fixed)
    return pl.pallas_call(
        functools.partial(step_kernel, cycle, parity, dot),
        out_shape=tuple(kept_shape(v.shape, v.dtype) for v in out_shape),
        in_specs=vmem_specs(count + len(stores)),
        out_specs=tuple(vmem_specs(len(out_shape))),
        input_output_aliases={count + i: i for i in range(len(stores))},
        compiler_params=pltpu.CompilerParams(vmem_limit_bytes=STEP_LIMIT),
    )(in_vmem(given), *[in_vmem(v) for v in fixed], *[in_vmem(v) for v in stores])


def block_of(cycle, depth):
    return cycle - depth // 2 * (LAG_EVEN + LAG_ODD) - depth % 2 * LAG_ODD


def span_of(last):
    if last < 12:
        return (0, 4) if last < 4 else (0, 12)
    return (6, 18) if last < 18 else (12, 24)


def run_chain(prepared):
    fixed, stores, given = prepared[:9], prepared[9:12], prepared[12]
    blocks = fixed[0].shape[0]
    sections = lax.axis_size("pipe")
    waiting = {0: [given] * LAG_EVEN, 1: [given] * LAG_ODD}
    cycles = sections // 2 * (LAG_EVEN + LAG_ODD) + blocks
    for cycle in range(cycles):
        for parity in (0, 1):
            senders = [
                depth
                for depth in range(parity, sections, 2)
                if 0 <= block_of(cycle, depth) < blocks
            ]
            came = waiting[parity].pop(0)
            if not senders:
                waiting[1 - parity].append(came)
                continue
            first, last = span_of(senders[-1])
            depths = range(first + parity, min(last, sections - 1), 2)
            pairs = [(sections - 1 - d, sections - 2 - d) for d in depths]
            if senders[0] >= sections - 1:
                pairs = []
            dot = turned_dot if cycle == 0 else plain_dot
            results = run_step(cycle, parity, dot, came, fixed, stores, len(pairs) > 0)
            stores = results[:3]
            if cycle == 0:
                held, *mats = turn_mats(*fixed[-2:], stores[2])
                fixed, stores = fixed[:-2] + tuple(mats), stores[:2] + (held,)
            if pairs:
                came = lax.ppermute(results[3], "pipe", pairs)
            waiting[1 - parity].append(came)
    return tuple(stores)


def grads_kernel(rows_ref, pres_ref, hidden_ref, outs_ref, keep_ref, send_ref):
    experts, blocks, cap, features = outs_ref.shape
    chunk = keep_ref.shape[2]
    tile = max(256, 2 * chunk)
    core = lax.axis_index("dp") % 2
    terms = []
    for e in range(experts):
        terms.append((rows_ref[e], pres_ref[e].reshape(blocks * cap, -1)))
    for e in range(experts):
        terms.append((outs_ref[e].reshape(blocks * cap, features), hidden_ref[e]))
    for number, (left, right) in enumerate(terms):
        for start in range(0, features, tile):
            part = lax.dot_general(
                left[:, start : start + tile],
                right,
                (((0,), (0,)), ((), ())),
                preferred_element_type=F32,
            ).astype(BF16)
            for pair in range(tile // (2 * chunk)):
                place = start // (2 * chunk) + pair
                low = part[2 * pair * chunk : (2 * pair + 1) * chunk]
                high = part[(2 * pair + 1) * chunk : (2 * pair + 2) * chunk]
                keep_ref[place, number] = jnp.where(core == 0, low, high)
                send_ref[place, number] = jnp.where(core == 0, high, low)


def expert_grads(rows, pres, hidden, outs, owners):
    experts, _, features = rows.shape
    width = pres.shape[-1]
    shape = (owners // 2, 2 * experts, features // owners, width)
    return pl.pallas_call(
        grads_kernel,
        out_shape=(kept_shape(shape, BF16),) * 2,
        in_specs=vmem_specs(4),
        out_specs=tuple(vmem_specs(2)),
        compiler_params=pltpu.CompilerParams(vmem_limit_bytes=VMEM_LIMIT),
    )(in_vmem(rows), in_vmem(pres), in_vmem(hidden), in_vmem(outs))


def split_x_kernel(along_x, keep_ref, came_ref, own_ref, *refs):
    far_right, far_left, near_right, near_left, next_ref, past_ref = refs
    my_x = lax.axis_index("dp") // 2 % along_x
    half = far_right.shape[1]
    for row in range(own_ref.shape[0]):
        parts = []
        for ahead in range(along_x):
            place = row * along_x + (my_x + ahead) % along_x
            part = keep_ref[place].astype(F32) + came_ref[place].astype(F32)
            parts.append(part.astype(BF16))
        own_ref[row] = parts[0]
        far_right[row] = parts[2][:half]
        far_left[row] = parts[2][half:]
        near_right[row] = parts[1][half:]
        near_left[row] = parts[3][:half]
        next_ref[row] = parts[1][:half]
        past_ref[row] = parts[3][half:]


def relay_kernel(next_ref, past_ref, from_left_ref, from_right_ref, right_ref, left_ref):
    right_ref[...] = (next_ref[...].astype(F32) + from_left_ref[...].astype(F32)).astype(BF16)
    left_ref[...] = (past_ref[...].astype(F32) + from_right_ref[...].astype(F32)).astype(BF16)


def split_y_kernel(own_ref, first_left, first_right, left_ref, right_ref, *part_refs):
    along_y = len(part_refs)
    half = left_ref.shape[1]
    my_y = lax.axis_index("dp") // (lax.axis_size("dp") // along_y)
    for ahead, part_ref in enumerate(part_refs):
        row = (my_y + ahead) % along_y
        low = left_ref[row].astype(F32) + first_right[row].astype(F32)
        high = right_ref[row].astype(F32) + first_left[row].astype(F32)
        total = own_ref[row].astype(F32)
        part_ref[:half] = (total[:half] + low).astype(part_ref.dtype)
        part_ref[half:] = (total[half:] + high).astype(part_ref.dtype)


def finish_kernel(own_ref, *refs):
    came_refs, (up_ref, down_ref) = refs[:-2], refs[-2:]
    experts = up_ref.shape[0]
    for number in range(2 * experts):
        total = own_ref[number]
        for came_ref in came_refs:
            total = total + came_ref[number].astype(F32)
        if number < experts:
            up_ref[number] = total
        else:
            down_ref[number - experts] = total


def call_in_vmem(kernel, out_shape, *values):
    return pl.pallas_call(
        kernel,
        out_shape=out_shape,
        in_specs=vmem_specs(len(values)),
        out_specs=tuple(vmem_specs(len(out_shape))),
        compiler_params=pltpu.CompilerParams(vmem_limit_bytes=VMEM_LIMIT),
    )(*[in_vmem(v) for v in values])


def reduce_to_owner(keep, send):
    owners = lax.axis_size("dp")
    along_x = 4
    along_y = owners // (2 * along_x)
    _, terms, chunk, width = keep.shape

    def move_x(ahead):
        return [
            (d, d - 2 * (d // 2 % along_x) + 2 * ((d // 2 + ahead) % along_x)) for d in range(owners)
        ]

    def move_y(ahead):
        return [(d, (d + ahead * 2 * along_x) % owners) for d in range(owners)]

    came = lax.ppermute(send, "dp", [(d, d ^ 1) for d in range(owners)])
    half = terms // 2
    whole = kept_shape((along_y, terms, chunk, width), BF16)
    single = kept_shape((along_y, half, chunk, width), BF16)
    own, far_right, far_left, near_right, near_left, following, past = call_in_vmem(
        functools.partial(split_x_kernel, along_x), (whole,) + (single,) * 6, keep, came
    )
    relay_left = lax.ppermute(far_right, "dp", move_x(1))
    relay_right = lax.ppermute(far_left, "dp", move_x(-1))
    first_left = lax.ppermute(near_right, "dp", move_x(1))
    first_right = lax.ppermute(near_left, "dp", move_x(-1))
    right, left = call_in_vmem(
        relay_kernel, (single, single), following, past, relay_left, relay_right
    )
    last_left = lax.ppermute(right, "dp", move_x(1))
    last_right = lax.ppermute(left, "dp", move_x(-1))
    shape = (terms, chunk, width)
    shapes = (kept_shape(shape, F32),) + (kept_shape(shape, BF16),) * (along_y - 1)
    own, *others = call_in_vmem(
        split_y_kernel, shapes, own, first_left, first_right, last_left, last_right
    )
    others = [lax.ppermute(v, "dp", move_y(i + 1)) for i, v in enumerate(others)]
    shapes = (jax.ShapeDtypeStruct((half, chunk, width), F32),) * 2
    up_shard, down_shard = call_in_vmem(finish_kernel, shapes, own, *others)
    return up_shard, jnp.swapaxes(down_shard, 1, 2)


def per_device(
    activations, out_grad, w_up, w_down, mod_scale, mod_gate, expert_ids, gate_prob, bucket
):
    features = activations.shape[2]
    prepared = prepare(
        activations[0],
        expert_ids[0].T,
        gate_prob[0].T,
        bucket[None, :],
        mod_scale[0],
        mod_gate[0],
        w_up[0],
        w_down[0],
        out_grad,
    )
    grads, outs, pres = run_chain(prepared)
    hidden, rows = prepared[13:]
    keep, send = expert_grads(rows, pres, hidden, outs, lax.axis_size("dp"))
    up_shard, down_shard = reduce_to_owner(keep, send)
    return (grads.reshape(1, -1, features), up_shard[None], down_shard[None])


def solution(mesh):
    return jax.shard_map(
        per_device,
        mesh=mesh,
        in_specs=(
            P("pipe", "dp", None),
            P("dp", None),
            P("pipe", None, None, None),
            P("pipe", None, None, None),
            P("pipe", None, None),
            P("pipe", None, None),
            P("pipe", "dp", None),
            P("pipe", "dp", None),
            P("dp"),
        ),
        out_specs=(P("pipe", "dp", None), P("pipe", None, "dp", None), P("pipe", None, None, "dp")),
        check_vma=False,
    )
```

```python
import functools

import jax
import jax.numpy as jnp
from jax import lax
from jax.experimental import pallas as pl
from jax.experimental.pallas import tpu as pltpu
from jax.sharding import PartitionSpec as P

TOK_MB = 64
CAP = 16
EPSILON = 1e-06
F32 = jnp.float32
BF16 = jnp.bfloat16
VMEM_LIMIT = 24 * 1024 * 1024
LAG_EVEN = 2
LAG_ODD = 1
STEP_LIMIT = 6 * 1024 * 1024


def in_vmem(value):
    return pltpu.with_memory_space_constraint(value, pltpu.VMEM)


def kept_shape(shape, dtype):
    return pltpu.VMEM(shape, dtype)


def vmem_specs(count):
    return [pl.BlockSpec(memory_space=pltpu.VMEM)] * count


def three_parts(table):
    high = table.astype(BF16)
    rest = table - high.astype(F32)
    middle = rest.astype(BF16)
    low = (rest - middle.astype(F32)).astype(BF16)
    return jnp.concatenate([high, middle, low], axis=0)


def prepare_kernel(
    act_hbm,
    ids_hbm,
    prob_hbm,
    bucket_hbm,
    scale_hbm,
    gate_hbm,
    up_hbm,
    down_hbm,
    top_hbm,
    top_ref,
    take_ref,
    place_ref,
    gate_ref,
    scale_ref,
    normed_ref,
    slope_ref,
    down_ref,
    up_ref,
    _grad_store,
    _outs_store,
    _pres_store,
    _given,
    hidden_ref,
    rows_ref,
    act_ref,
    ids_ref,
    prob_ref,
    bucket_ref,
    scale_table_ref,
    gate_table_ref,
    sems,
):
    moves = [
        (ids_hbm, ids_ref),
        (prob_hbm, prob_ref),
        (bucket_hbm, bucket_ref),
        (scale_hbm, scale_table_ref),
        (gate_hbm, gate_table_ref),
        (act_hbm, act_ref),
        (up_hbm, up_ref),
        (top_hbm, top_ref),
        (down_hbm, down_ref),
    ]
    copies = [
        pltpu.make_async_copy(source, target, sems.at[number])
        for number, (source, target) in enumerate(moves)
    ]
    for copy in copies:
        copy.start()
    for copy in copies[:3]:
        copy.wait()
    tokens = act_ref.shape[0]
    experts = up_ref.shape[0]
    slots = experts * CAP
    features = act_ref.shape[1]
    ids = ids_ref[...]
    prob = prob_ref[...]
    bucket = bucket_ref[...].astype(F32)
    lane = lax.broadcasted_iota(jnp.int32, (1, tokens), 1) % TOK_MB
    slot_no = (lax.broadcasted_iota(jnp.int32, (CAP, tokens), 0) + 1).astype(F32)
    hits = []
    gates = []
    for expert in range(experts):
        chosen = ids == expert
        routed = jnp.max(jnp.where(chosen, 1.0, 0.0), axis=0, keepdims=True)
        token_gate = jnp.sum(jnp.where(chosen, prob, 0.0), axis=0, keepdims=True)
        place = routed
        step = 1
        while step < TOK_MB:
            place = place + jnp.where(lane >= step, pltpu.roll(place, step, 1), 0.0)
            step *= 2
        hit = jnp.where((place == slot_no) & (routed > 0.0), 1.0, 0.0)
        hits.append(hit)
        gates.append(hit * token_gate)
    take = jnp.concatenate(hits, axis=0)
    gates = jnp.concatenate(gates, axis=0)
    buckets = take * bucket
    for copy in copies[3:6]:
        copy.wait()
    tables = three_parts(scale_table_ref[...]), three_parts(gate_table_ref[...])
    entries = scale_table_ref.shape[0]
    wide = lax.broadcasted_iota(jnp.int32, (slots, 2 * TOK_MB), 1)
    eye = jnp.where(
        lax.broadcasted_iota(jnp.int32, (TOK_MB, 2 * TOK_MB), 0)
        == lax.broadcasted_iota(jnp.int32, (TOK_MB, 2 * TOK_MB), 1),
        1.0,
        0.0,
    )
    entry_no = lax.broadcasted_iota(jnp.int32, (slots, 3 * entries), 1) % entries
    for block in range(tokens // TOK_MB):
        pair = slice(block // 2 * 2 * TOK_MB, (block // 2 + 1) * 2 * TOK_MB)
        inside = (wide < TOK_MB) if block % 2 == 0 else (wide >= TOK_MB)
        block_take = jnp.where(inside, take[:, pair], 0.0)
        slot_gate = jnp.sum(jnp.where(inside, gates[:, pair], 0.0), axis=1, keepdims=True)
        slot_bucket = jnp.sum(jnp.where(inside, buckets[:, pair], 0.0), axis=1, keepdims=True)
        raw = jnp.dot(block_take.astype(BF16), act_ref[pair, :], preferred_element_type=F32)
        first = block_take if block % 2 == 0 else pltpu.roll(block_take, TOK_MB, 1)
        take_ref[block] = first.astype(BF16)
        stacked = jnp.concatenate([first, first, eye], axis=0)
        place_ref[block] = jnp.transpose(stacked)[:TOK_MB, :].astype(BF16)
        picked = jnp.where(slot_bucket.astype(jnp.int32) == entry_no, 1.0, 0.0).astype(BF16)
        scale_rows = 1.0 + jnp.dot(picked, tables[0], preferred_element_type=F32)
        gate_rows = jnp.dot(picked, tables[1], preferred_element_type=F32)
        gate_ref[block] = slot_gate * gate_rows
        centred = raw - jnp.mean(raw, axis=-1, keepdims=True)
        inv_std = lax.rsqrt(jnp.mean(centred * centred, axis=-1, keepdims=True) + EPSILON)
        normed = centred * inv_std
        normed_ref[block] = normed
        scale_ref[block] = scale_rows * inv_std
        inputs = (normed * scale_rows).astype(BF16)
        for expert in range(experts):
            rows_ref[expert, block * CAP : (block + 1) * CAP, :] = inputs[
                expert * CAP : (expert + 1) * CAP, :
            ]
    copies[6].wait()
    for expert in range(experts):
        pre_act = jnp.dot(rows_ref[expert], up_ref[expert], preferred_element_type=F32)
        root = 0.7978845608028654
        square = pre_act * pre_act
        bend = jnp.tanh(root * (pre_act + 0.044715 * (square * pre_act)))
        half = 0.5 * (1.0 + bend)
        hidden_ref[expert] = (pre_act * half).astype(BF16)
        slope = half + 0.5 * pre_act * (1.0 - bend * bend) * (root * (1.0 + 0.134145 * square))
        slope_ref[expert] = slope.reshape(slope_ref.shape[1:])
    for copy in copies[7:]:
        copy.wait()


def prepare(act, ids, prob, bucket, scale_table, gate_table, up_mats, down_mats, out_grad):
    tokens, features = act.shape
    experts, _, width = up_mats.shape
    blocks = tokens // TOK_MB
    slots = experts * CAP
    top = out_grad.reshape(blocks, TOK_MB, features)
    values = (act, ids, prob, bucket, scale_table, gate_table, up_mats, down_mats, top)
    out_shape = (
        kept_shape(top.shape, BF16),
        kept_shape((blocks, slots, 2 * TOK_MB), BF16),
        kept_shape((blocks, TOK_MB, 2 * slots + TOK_MB), BF16),
        kept_shape((blocks, slots, features), F32),
        kept_shape((blocks, slots, features), F32),
        kept_shape((blocks, slots, features), F32),
        kept_shape((experts, blocks, CAP, width), F32),
        kept_shape(down_mats.shape, BF16),
        kept_shape(up_mats.shape, BF16),
        kept_shape((blocks, TOK_MB, features), BF16),
        kept_shape((experts, blocks, CAP, features), BF16),
        kept_shape((experts, blocks, CAP, width), BF16),
        kept_shape((TOK_MB, features), BF16),
        kept_shape((experts, blocks * CAP, width), BF16),
        kept_shape((experts, blocks * CAP, features), BF16),
    )
    return pl.pallas_call(
        prepare_kernel,
        out_shape=out_shape,
        in_specs=[pl.BlockSpec(memory_space=pltpu.HBM)] * len(values),
        out_specs=tuple(vmem_specs(len(out_shape))),
        scratch_shapes=[pltpu.VMEM(v.shape, v.dtype) for v in values[:6]]
        + [pltpu.SemaphoreType.DMA((len(values),))],
        compiler_params=pltpu.CompilerParams(vmem_limit_bytes=VMEM_LIMIT),
    )(*[pltpu.with_memory_space_constraint(v, pltpu.HBM) for v in values])


def step_kernel(
    cycle,
    parity,
    dot,
    given_ref,
    top_ref,
    take_ref,
    place_ref,
    gate_ref,
    scale_ref,
    normed_ref,
    slope_ref,
    down_ref,
    up_ref,
    _grad_in,
    _outs_in,
    _pres_in,
    grad_ref,
    outs_ref,
    pres_ref,
    *sent_refs,
):
    experts = down_ref.shape[0]
    blocks = take_ref.shape[0]
    depth = lax.axis_size("pipe") - 1 - lax.axis_index("pipe")
    block = block_of(cycle, depth)

    @pl.when((depth % 2 == parity) & (block >= 0) & (block < blocks))
    def _():
        grad_out = jnp.where(depth == 0, top_ref[block], given_ref[...])
        gathered = jnp.dot(take_ref[block][:, :TOK_MB], grad_out, preferred_element_type=F32)
        outs = (gate_ref[block] * gathered).astype(BF16)
        back = []
        for expert in range(experts):
            rows = slice(expert * CAP, (expert + 1) * CAP)
            outs_ref[expert, block] = outs[rows, :]
            hid_grad = dot(outs[rows, :], down_ref[expert])
            pres = (hid_grad * slope_ref[expert, block]).astype(BF16)
            pres_ref[expert, block] = pres
            back.append(dot(pres, up_ref[expert]))
        varied = jnp.concatenate(back, axis=0) * scale_ref[block]
        normed = normed_ref[block]
        lifted = (
            varied
            - jnp.mean(varied, axis=-1, keepdims=True)
            - normed * jnp.mean(varied * normed, axis=-1, keepdims=True)
        )
        high = lifted.astype(BF16)
        low = (lifted - high.astype(F32)).astype(BF16)
        parts = jnp.concatenate([high, low, grad_out], axis=0)
        grad_in = jnp.dot(place_ref[block], parts, preferred_element_type=F32).astype(BF16)
        for sent_ref in sent_refs:
            sent_ref[...] = grad_in
        grad_ref[block] = grad_in


def turned_dot(left, right):
    return lax.dot_general(left, right, (((1,), (1,)), ((), ())), preferred_element_type=F32)


def plain_dot(left, right):
    return jnp.dot(left, right, preferred_element_type=F32)


def turn_kernel(down_ref, up_ref, _pres_in, pres_ref, down_turned, up_turned):
    for source, target in ((down_ref, down_turned), (up_ref, up_turned)):
        for expert in range(source.shape[0]):
            target[expert] = jnp.transpose(source[expert])


def turn_mats(down_mats, up_mats, held):
    experts, width, features = down_mats.shape
    return pl.pallas_call(
        turn_kernel,
        out_shape=(
            kept_shape(held.shape, held.dtype),
            kept_shape((experts, features, width), BF16),
            kept_shape((experts, width, features), BF16),
        ),
        in_specs=vmem_specs(3),
        out_specs=tuple(vmem_specs(3)),
        input_output_aliases={2: 0},
        compiler_params=pltpu.CompilerParams(vmem_limit_bytes=VMEM_LIMIT),
    )(in_vmem(down_mats), in_vmem(up_mats), in_vmem(held))


def run_step(cycle, parity, dot, given, fixed, stores, sends):
    out_shape = stores + (given,) * sends
    count = 1 + len(fixed)
    return pl.pallas_call(
        functools.partial(step_kernel, cycle, parity, dot),
        out_shape=tuple(kept_shape(v.shape, v.dtype) for v in out_shape),
        in_specs=vmem_specs(count + len(stores)),
        out_specs=tuple(vmem_specs(len(out_shape))),
        input_output_aliases={count + i: i for i in range(len(stores))},
        compiler_params=pltpu.CompilerParams(vmem_limit_bytes=STEP_LIMIT),
    )(in_vmem(given), *[in_vmem(v) for v in fixed], *[in_vmem(v) for v in stores])


def block_of(cycle, depth):
    return cycle - depth // 2 * (LAG_EVEN + LAG_ODD) - depth % 2 * LAG_ODD


def span_of(last):
    if last < 12:
        return (0, 4) if last < 4 else (0, 12)
    return (6, 18) if last < 18 else (12, 24)


def run_chain(prepared):
    fixed, stores, given = prepared[:9], prepared[9:12], prepared[12]
    blocks = fixed[0].shape[0]
    sections = lax.axis_size("pipe")
    waiting = {0: [given] * LAG_EVEN, 1: [given] * LAG_ODD}
    cycles = sections // 2 * (LAG_EVEN + LAG_ODD) + blocks
    for cycle in range(cycles):
        for parity in (0, 1):
            senders = [
                depth
                for depth in range(parity, sections, 2)
                if 0 <= block_of(cycle, depth) < blocks
            ]
            came = waiting[parity].pop(0)
            if not senders:
                waiting[1 - parity].append(came)
                continue
            first, last = span_of(senders[-1])
            depths = range(first + parity, min(last, sections - 1), 2)
            pairs = [(sections - 1 - d, sections - 2 - d) for d in depths]
            if senders[0] >= sections - 1:
                pairs = []
            dot = turned_dot if cycle == 0 else plain_dot
            results = run_step(cycle, parity, dot, came, fixed, stores, len(pairs) > 0)
            stores = results[:3]
            if cycle == 0:
                held, *mats = turn_mats(*fixed[-2:], stores[2])
                fixed, stores = fixed[:-2] + tuple(mats), stores[:2] + (held,)
            if pairs:
                came = lax.ppermute(results[3], "pipe", pairs)
            waiting[1 - parity].append(came)
    return tuple(stores)


def grads_kernel(rows_ref, pres_ref, hidden_ref, outs_ref, keep_ref, send_ref):
    experts, blocks, cap, features = outs_ref.shape
    chunk = keep_ref.shape[2]
    tile = max(256, 2 * chunk)
    core = lax.axis_index("dp") % 2
    terms = []
    for e in range(experts):
        terms.append((rows_ref[e], pres_ref[e].reshape(blocks * cap, -1)))
    for e in range(experts):
        terms.append((outs_ref[e].reshape(blocks * cap, features), hidden_ref[e]))
    for number, (left, right) in enumerate(terms):
        for start in range(0, features, tile):
            part = lax.dot_general(
                left[:, start : start + tile],
                right,
                (((0,), (0,)), ((), ())),
                preferred_element_type=F32,
            ).astype(BF16)
            for pair in range(tile // (2 * chunk)):
                place = start // (2 * chunk) + pair
                low = part[2 * pair * chunk : (2 * pair + 1) * chunk]
                high = part[(2 * pair + 1) * chunk : (2 * pair + 2) * chunk]
                keep_ref[place, number] = jnp.where(core == 0, low, high)
                send_ref[place, number] = jnp.where(core == 0, high, low)


def expert_grads(rows, pres, hidden, outs, owners):
    experts, _, features = rows.shape
    width = pres.shape[-1]
    shape = (owners // 2, 2 * experts, features // owners, width)
    return pl.pallas_call(
        grads_kernel,
        out_shape=(kept_shape(shape, BF16),) * 2,
        in_specs=vmem_specs(4),
        out_specs=tuple(vmem_specs(2)),
        compiler_params=pltpu.CompilerParams(vmem_limit_bytes=VMEM_LIMIT),
    )(in_vmem(rows), in_vmem(pres), in_vmem(hidden), in_vmem(outs))


def split_x_kernel(along_x, keep_ref, came_ref, own_ref, *refs):
    far_right, far_left, near_right, near_left, next_ref, past_ref = refs
    my_x = lax.axis_index("dp") // 2 % along_x
    half = far_right.shape[1]
    for row in range(own_ref.shape[0]):
        parts = []
        for ahead in range(along_x):
            place = row * along_x + (my_x + ahead) % along_x
            part = keep_ref[place].astype(F32) + came_ref[place].astype(F32)
            parts.append(part.astype(BF16))
        own_ref[row] = parts[0]
        far_right[row] = parts[2][:half]
        far_left[row] = parts[2][half:]
        near_right[row] = parts[1][half:]
        near_left[row] = parts[3][:half]
        next_ref[row] = parts[1][:half]
        past_ref[row] = parts[3][half:]


def relay_kernel(next_ref, past_ref, from_left_ref, from_right_ref, right_ref, left_ref):
    right_ref[...] = (next_ref[...].astype(F32) + from_left_ref[...].astype(F32)).astype(BF16)
    left_ref[...] = (past_ref[...].astype(F32) + from_right_ref[...].astype(F32)).astype(BF16)


def far_first(count):
    return [0] + sorted(range(1, count), key=lambda a: -min(a, count - a))


def split_y_kernel(own_ref, first_left, first_right, left_ref, right_ref, *part_refs):
    along_y = len(part_refs)
    half = left_ref.shape[1]
    my_y = lax.axis_index("dp") // (lax.axis_size("dp") // along_y)
    for ahead, part_ref in zip(far_first(along_y), part_refs):
        row = (my_y + ahead) % along_y
        low = left_ref[row].astype(F32) + first_right[row].astype(F32)
        high = right_ref[row].astype(F32) + first_left[row].astype(F32)
        total = own_ref[row].astype(F32)
        part_ref[:half] = (total[:half] + low).astype(part_ref.dtype)
        part_ref[half:] = (total[half:] + high).astype(part_ref.dtype)


def finish_kernel(own_ref, *refs):
    came_refs, (up_ref, down_ref) = refs[:-2], refs[-2:]
    experts = up_ref.shape[0]
    for number in range(2 * experts):
        total = own_ref[number]
        for came_ref in came_refs:
            total = total + came_ref[number].astype(F32)
        if number < experts:
            up_ref[number] = total
        else:
            down_ref[number - experts] = total


def call_in_vmem(kernel, out_shape, *values):
    return pl.pallas_call(
        kernel,
        out_shape=out_shape,
        in_specs=vmem_specs(len(values)),
        out_specs=tuple(vmem_specs(len(out_shape))),
        compiler_params=pltpu.CompilerParams(vmem_limit_bytes=VMEM_LIMIT),
    )(*[in_vmem(v) for v in values])


def reduce_to_owner(keep, send):
    owners = lax.axis_size("dp")
    along_x = 4
    along_y = owners // (2 * along_x)
    _, terms, chunk, width = keep.shape

    def move_x(ahead):
        return [
            (d, d - 2 * (d // 2 % along_x) + 2 * ((d // 2 + ahead) % along_x)) for d in range(owners)
        ]

    def move_y(ahead):
        return [(d, (d + ahead * 2 * along_x) % owners) for d in range(owners)]

    came = lax.ppermute(send, "dp", [(d, d ^ 1) for d in range(owners)])
    half = terms // 2
    whole = kept_shape((along_y, terms, chunk, width), BF16)
    single = kept_shape((along_y, half, chunk, width), BF16)
    own, far_right, far_left, near_right, near_left, following, past = call_in_vmem(
        functools.partial(split_x_kernel, along_x), (whole,) + (single,) * 6, keep, came
    )
    relay_left = lax.ppermute(far_right, "dp", move_x(1))
    relay_right = lax.ppermute(far_left, "dp", move_x(-1))
    first_left = lax.ppermute(near_right, "dp", move_x(1))
    first_right = lax.ppermute(near_left, "dp", move_x(-1))
    right, left = call_in_vmem(
        relay_kernel, (single, single), following, past, relay_left, relay_right
    )
    last_left = lax.ppermute(right, "dp", move_x(1))
    last_right = lax.ppermute(left, "dp", move_x(-1))
    shape = (terms, chunk, width)
    shapes = (kept_shape(shape, F32),) + (kept_shape(shape, BF16),) * (along_y - 1)
    own, *others = call_in_vmem(
        split_y_kernel, shapes, own, first_left, first_right, last_left, last_right
    )
    order = far_first(along_y)[1:]
    others = [lax.ppermute(v, "dp", move_y(a)) for a, v in zip(order, others)]
    shapes = (jax.ShapeDtypeStruct((half, chunk, width), F32),) * 2
    up_shard, down_shard = call_in_vmem(finish_kernel, shapes, own, *others)
    return up_shard, jnp.swapaxes(down_shard, 1, 2)


def per_device(
    activations, out_grad, w_up, w_down, mod_scale, mod_gate, expert_ids, gate_prob, bucket
):
    features = activations.shape[2]
    prepared = prepare(
        activations[0],
        expert_ids[0].T,
        gate_prob[0].T,
        bucket[None, :],
        mod_scale[0],
        mod_gate[0],
        w_up[0],
        w_down[0],
        out_grad,
    )
    grads, outs, pres = run_chain(prepared)
    hidden, rows = prepared[13:]
    keep, send = expert_grads(rows, pres, hidden, outs, lax.axis_size("dp"))
    up_shard, down_shard = reduce_to_owner(keep, send)
    return (grads.reshape(1, -1, features), up_shard[None], down_shard[None])


def solution(mesh):
    return jax.shard_map(
        per_device,
        mesh=mesh,
        in_specs=(
            P("pipe", "dp", None),
            P("dp", None),
            P("pipe", None, None, None),
            P("pipe", None, None, None),
            P("pipe", None, None),
            P("pipe", None, None),
            P("pipe", "dp", None),
            P("pipe", "dp", None),
            P("dp"),
        ),
        out_specs=(P("pipe", "dp", None), P("pipe", None, "dp", None), P("pipe", None, None, "dp")),
        check_vma=False,
    )
```
